128 devices in a mesh: rep: 32 (over y, x_hi, z), shard: 4 (over x_lo, core).
Axes of the slice: x: 4 (x_hi: 2, x_lo: 2; x = x_hi * 2 + x_lo), y: 4, z: 4, core: 2. Of those that a mesh axis runs over, the one named last changes fastest.
Arguments:
- hidden_in: bfloat16 [32, 2048, 1024], P('rep', 'shard'), may hold values from -6 to 6
- cotangent: bfloat16 [32, 2048, 1024], P('rep', 'shard'), may hold values from -6 to 6
- in_weight: float32 [1024, 4384], P('shard'), may hold values from -0.1875 to 0.1875
- in_first: float32 [1024, 4384], P('shard'), may hold values from -80 to 80
- in_second: float32 [1024, 4384], P('shard'), may hold values from 8.192 to 131.072
- out_weight: float32 [2048, 1024], P('shard'), may hold values from -0.125 to 0.125
- out_first: float32 [2048, 1024], P('shard'), may hold values from -160 to 160
- out_second: float32 [2048, 1024], P('shard'), may hold values from 32.768 to 524.288
- conv_weight: float32 [5, 2304], P(None, 'shard'), may hold values from -3 to 3
- conv_first: float32 [5, 2304], P(None, 'shard'), may hold values from -80 to 80
- conv_second: float32 [5, 2304], P(None, 'shard'), may hold values from 8.192 to 131.072
- norm_gains: float32 [3072], P('shard'), may hold values from 0.5 to 1.5
- gains_first: float32 [3072], P('shard'), may hold values from -160 to 160
- gains_second: float32 [3072], P('shard'), may hold values from 32.768 to 524.288
- head_params: float32 [3, 32], P(None, 'shard'), may hold values from -6.1 to 2, as said below
- head_first: float32 [3, 32], P(None, 'shard'), may hold values from -640 to 640
- head_second: float32 [3, 32], P(None, 'shard'), may hold values from 524.288 to 8388.608
Outputs:
- block_out: bfloat16 [32, 2048, 1024], P('rep', 'shard')
- grad_input: float32 [32, 2048, 1024], P('rep', 'shard')
- in_weight_new: float32 [1024, 4384], P('shard')
- in_first_new: float32 [1024, 4384], P('shard')
- in_second_new: float32 [1024, 4384], P('shard')
- out_weight_new: float32 [2048, 1024], P('shard')
- out_first_new: float32 [2048, 1024], P('shard')
- out_second_new: float32 [2048, 1024], P('shard')
- conv_weight_new: float32 [5, 2304], P(None, 'shard')
- conv_first_new: float32 [5, 2304], P(None, 'shard')
- conv_second_new: float32 [5, 2304], P(None, 'shard')
- gains_new: float32 [3072], P('shard')
- gains_first_new: float32 [3072], P('shard')
- gains_second_new: float32 [3072], P('shard')
- head_params_new: float32 [3, 32], P(None, 'shard')
- head_first_new: float32 [3, 32], P(None, 'shard')
- head_second_new: float32 [3, 32], P(None, 'shard')
The draws below stay inside these ranges and needn't reach their ends.
Inputs may be any that keep to these rules, and one draw needn't show every extreme that they name: `head_params`: row 0 lies in -4.5 to -3.5, row 2 in 0.5 to 2.
All inputs are finite; a program needn't handle non-finite values.
Results may differ from the reference program's by a relative error of at most 0.0025.
The reference program's roundings to bfloat16 on the way count: a program that leaves them out, or rounds other values in their place, can miss the bound.
Values may be sent and summed in bfloat16 or wider, within the bound.
A program may use at most 256 MiB of HBM per device.

```python
import math
import jax
import jax.numpy as jnp
from jax import lax

D = 1024
DI = 2048
P_SIZE = 64
N = 128
KCONV = 4
STEP = 10
H = 32
CONV = 2304
E = 4384
LENGTH = 2048
SEQS = 32
TOKENS = 65536


def draw_head_params(key, part):
    key = jax.random.fold_in(key, 7)
    subkeys = jax.random.split(key, 3)
    bias_row = jax.random.uniform(subkeys[0], (H,), jnp.float32, -4.5, -3.5)
    rate_row = jnp.exp(jax.random.uniform(subkeys[1], (H,), jnp.float32, math.log(0.5 / LENGTH), math.log(1.0 / 30.0)))
    skip_row = jax.random.uniform(subkeys[2], (H,), jnp.float32, 0.5, 1.5)
    return jnp.stack([bias_row, jnp.log(rate_row / 0.03), skip_row])


def levels(rng, dims, cuts, smallest, high):
    def one(axis_at, parts):
        heights = jax.random.uniform(jax.random.fold_in(jax.random.fold_in(rng, 6), axis_at), (parts,), jnp.float32, smallest / len(cuts), high / len(cuts))
        return jnp.repeat(jnp.exp(heights), dims[axis_at] // parts).reshape((-1,) + (1,) * (len(dims) - axis_at - 1))

    factor_of = one(*cuts[0])
    for cut in cuts[1:]:
        factor_of = factor_of * one(*cut)
    return factor_of


def scatter_about(key, dims, scale, limit, shards=(), kind=jnp.bfloat16):
    loudness = levels(key, dims, shards, -0.22, 0.18) if shards else 1.0
    drawn = jax.random.normal(key, dims, jnp.float32) * scale * loudness
    return jnp.minimum(jnp.maximum(drawn, -limit), limit).astype(kind)


def setup_inputs(seed: int = 0) -> dict:
    seeds = jax.random.split(jax.random.key(seed), 18)
    hidden_in = scatter_about(seeds[0], (SEQS, LENGTH, D), 1.0, 6.0, ((0, 32), (1, 4)))
    cotangent = scatter_about(seeds[1], (SEQS, LENGTH, D), 1.0, 6.0, ((0, 32), (1, 4)))
    in_weight = scatter_about(seeds[2], (D, E), D ** -0.5, 0.1875, ((0, 4),), jnp.float32)
    in_first = scatter_about(seeds[3], (D, E), (0.05 * TOKENS ** 0.5), 80.0, ((0, 4),), jnp.float32)
    in_second = jnp.clip(jnp.exp(math.log(131.072) - 2.7725887 * jax.random.uniform(seeds[4], (D, E), jnp.float32) ** levels(seeds[4], (D, E), ((0, 4),), -0.2, 0.2)), 8.192, 131.072)
    out_weight = scatter_about(seeds[5], (DI, D), DI ** -0.5, 0.125, ((0, 4),), jnp.float32)
    out_first = scatter_about(seeds[6], (DI, D), (0.1 * TOKENS ** 0.5), 160.0, ((0, 4),), jnp.float32)
    out_second = jnp.clip(jnp.exp(math.log(524.288) - 2.7725887 * jax.random.uniform(seeds[7], (DI, D), jnp.float32) ** levels(seeds[7], (DI, D), ((0, 4),), -0.2, 0.2)), 32.768, 524.288)
    conv_weight = scatter_about(seeds[8], (KCONV + 1, CONV), KCONV ** -0.5, 3.0, ((1, 4),), jnp.float32)
    conv_first = scatter_about(seeds[9], (KCONV + 1, CONV), (0.05 * TOKENS ** 0.5), 80.0, ((1, 4),), jnp.float32)
    conv_second = jnp.clip(jnp.exp(math.log(131.072) - 2.7725887 * jax.random.uniform(seeds[10], (KCONV + 1, CONV), jnp.float32) ** levels(seeds[10], (KCONV + 1, CONV), ((1, 4),), -0.2, 0.2)), 8.192, 131.072)
    norm_gains = jnp.clip(1.0 + 0.1 * jax.random.normal(seeds[11], (D + DI,), jnp.float32), 0.5, 1.5)
    gains_first = scatter_about(seeds[12], (D + DI,), (0.1 * TOKENS ** 0.5), 160.0, ((0, 4),), jnp.float32)
    gains_second = jnp.clip(jnp.exp(math.log(524.288) - 2.7725887 * jax.random.uniform(seeds[13], (D + DI,), jnp.float32) ** levels(seeds[13], (D + DI,), ((0, 4),), -0.2, 0.2)), 32.768, 524.288)
    head_params = draw_head_params(jax.random.fold_in(seeds[17], 71), 0)
    head_first = scatter_about(seeds[15], (3, H), (0.4 * TOKENS ** 0.5), 640.0, ((1, 4),), jnp.float32)
    head_second = jnp.clip(jnp.exp(math.log(8388.608) - 2.7725887 * jax.random.uniform(seeds[16], (3, H), jnp.float32) ** levels(seeds[16], (3, H), ((1, 4),), -0.2, 0.2)), 524.288, 8388.608)
    return {"hidden_in": hidden_in, "cotangent": cotangent, "in_weight": in_weight, "in_first": in_first, "in_second": in_second, "out_weight": out_weight, "out_first": out_first, "out_second": out_second, "conv_weight": conv_weight, "conv_first": conv_first, "conv_second": conv_second, "norm_gains": norm_gains, "gains_first": gains_first, "gains_second": gains_second, "head_params": head_params, "head_first": head_first, "head_second": head_second}


NORM_EPS = 1e-05
BETA_ONE = 0.9
BETA_TWO = 0.999
ADAM_EPS = 1e-08
PRECISE = lax.Precision.HIGHEST

@jax.custom_vjp
def low(v):
    return lax.optimization_barrier(v.astype(jnp.bfloat16)).astype(jnp.float32)

@jax.custom_vjp
def low_back(v):
    return v

def low_keep(v):
    return (low(v), None)

def low_pass(kept, grad):
    return (grad,)

def back_keep(v):
    return (v, None)

def back_low(kept, grad):
    return (low(grad),)
low.defvjp(low_keep, low_pass)
low_back.defvjp(back_keep, back_low)

def group_scan(inner_values, step_sizes, decay_rate, write_proj, read_proj, start_state):
    row_count = inner_values.shape[0]
    block_width = min(256, row_count)
    block_count = row_count // block_width
    pieces = (inner_values.reshape(block_count, block_width, H, P_SIZE), step_sizes.reshape(block_count, block_width, H), write_proj.reshape(block_count, block_width, N), read_proj.reshape(block_count, block_width, N))
    causal_mask = lax.broadcasted_iota(jnp.int32, (block_width, block_width), 0) >= lax.broadcasted_iota(jnp.int32, (block_width, block_width), 1)

    def advance(state_now, block_in):
        block_values, block_steps, block_write, block_read = block_in
        cumulative = jnp.cumsum(block_steps * decay_rate[None, :], axis=0)
        spread = cumulative.T[:, :, None] - cumulative.T[:, None, :]
        factor = jnp.where(causal_mask[None], jnp.exp(jnp.where(causal_mask[None], spread, 0.0)), 0.0)
        intersection = jnp.einsum('in,jn->ij', block_read, block_write, precision=PRECISE)
        scaled = block_values * block_steps[:, :, None]
        within = jnp.einsum('hij,jhp->ihp', factor * intersection[None], scaled, precision=PRECISE)
        carried = jnp.exp(cumulative)[:, :, None] * jnp.einsum('in,hpn->ihp', block_read, state_now, precision=PRECISE)
        remain = jnp.exp(cumulative[-1][None, :] - cumulative)
        renewed = jnp.exp(cumulative[-1])[:, None, None] * state_now + jnp.einsum('jhp,jn->hpn', scaled * remain[:, :, None], block_write, precision=PRECISE)
        return (renewed, within + carried)
    end_state, outputs = lax.scan(jax.checkpoint(advance), start_state, pieces)
    return (outputs.reshape(row_count, H, P_SIZE), end_state)

def conv_front(padded, conv_full, head_full, step_raw):
    tap_count = conv_full.shape[0] - 1
    row_count = padded.shape[0] - tap_count + 1
    conv_sum = conv_full[tap_count][None, :]
    for offset in range(tap_count):
        conv_sum = conv_sum + conv_full[offset][None, :] * padded[offset:offset + row_count]
    active = jax.nn.silu(conv_sum)
    inner_values = active[:, :DI].reshape(row_count, H, P_SIZE)
    write_proj = active[:, DI:DI + N]
    read_proj = active[:, DI + N:]
    step_sizes = jax.nn.softplus(step_raw + head_full[0][None, :])
    decay_rate = -jnp.exp(head_full[1])
    return (inner_values, write_proj, read_proj, step_sizes, decay_rate)

def forward(rows_f32, in_weight, out_weight, conv_weight, norm_gains, head_params):
    in_low = low(in_weight)
    out_low = low(out_weight)
    conv_low = low(conv_weight)
    gain_low = low(norm_gains)
    head_low = low(head_params)
    length = rows_f32.shape[0]
    square = lax.optimization_barrier(jnp.mean(rows_f32 * rows_f32, axis=-1, keepdims=True))
    normed_in = low(rows_f32 * lax.rsqrt(square + NORM_EPS) * gain_low[:D])
    projected = low_back(jnp.dot(normed_in, in_low, precision=PRECISE))
    gate_raw = projected[:, :DI]
    conv_in = low(projected[:, DI:DI + CONV])
    step_raw = projected[:, DI + CONV:]
    padded = jnp.concatenate([jnp.zeros((KCONV - 1, CONV), jnp.float32), conv_in], axis=0)
    inner_values, write_proj, read_proj, step_sizes, decay_rate = conv_front(padded, conv_low, head_low, step_raw)
    outputs, end_state = group_scan(inner_values, step_sizes, decay_rate, write_proj, read_proj, jnp.zeros((H, P_SIZE, N), jnp.float32))
    mixer_out = outputs + head_low[2][None, :, None] * inner_values
    flat_rows = mixer_out.reshape(length, DI) * jax.nn.silu(gate_raw)
    gated_rows = low(flat_rows * lax.rsqrt(lax.optimization_barrier(jnp.mean(flat_rows * flat_rows, axis=-1, keepdims=True)) + NORM_EPS) * gain_low[D:])
    return rows_f32 + jnp.dot(gated_rows, out_low, precision=PRECISE)

def adamw(weight, first_moment, second, gradient, step_rate, weight_decay):
    first_new = BETA_ONE * first_moment + (1.0 - BETA_ONE) * gradient
    second_new = BETA_TWO * second + (1.0 - BETA_TWO) * gradient * gradient
    first_hat = first_new / (1.0 - BETA_ONE ** STEP)
    second_hat = second_new / (1.0 - BETA_TWO ** STEP)
    weight_new = weight - step_rate * (first_hat / (jnp.sqrt(second_hat) + ADAM_EPS) + weight_decay * weight)
    return (weight_new, first_new, second_new)

def reference(hidden_in, cotangent, in_weight, in_first, in_second, out_weight, out_first, out_second, conv_weight, conv_first, conv_second, norm_gains, gains_first, gains_second, head_params, head_first, head_second):
    masters = (in_weight, out_weight, conv_weight, norm_gains, head_params)

    def one_sequence(totals, seq_pair):
        seq_rows, seq_cot = seq_pair
        result, pullback = jax.vjp(forward, seq_rows.astype(jnp.float32), in_weight, out_weight, conv_weight, norm_gains, head_params)
        gradients = pullback(seq_cot.astype(jnp.float32))
        totals = tuple((before + update for before, update in zip(totals, gradients[1:])))
        return (totals, (result.astype(jnp.bfloat16), gradients[0]))
    start = tuple((jnp.zeros_like(master) for master in masters))
    totals, outs_pair = lax.scan(one_sequence, start, (hidden_in, cotangent))
    block_out, grad_input = outs_pair
    in_new = adamw(in_weight, in_first, in_second, totals[0], 0.05, 0.1)
    out_new = adamw(out_weight, out_first, out_second, totals[1], 0.05, 0.1)
    conv_new = adamw(conv_weight, conv_first, conv_second, totals[2], 0.3, 0.1)
    gains_new = adamw(norm_gains, gains_first, gains_second, totals[3], 0.5, 0.0)
    head_new = adamw(head_params, head_first, head_second, totals[4], 1.0, 0.0)
    return (block_out, grad_input, in_new[0], in_new[1], in_new[2], out_new[0], out_new[1], out_new[2], conv_new[0], conv_new[1], conv_new[2], gains_new[0], gains_new[1], gains_new[2], head_new[0], head_new[1], head_new[2])
```

```python
import functools

import jax
import jax.numpy as jnp
from jax import lax
from jax.experimental import pallas as pl
from jax.experimental.pallas import tpu as pltpu
from jax.sharding import PartitionSpec as P

STEP = 10
BETA_ONE = 0.9
BETA_TWO = 0.999
ADAM_EPS = 1e-08
D = 1024
DI = 2048
P_SIZE = 64
N = 128
KCONV = 4
H = 32
CONV = 2304
NORM_EPS = 1e-05
Q = 128
CHUNKS = 4
TOK = Q * CHUNKS
HALO = 16
WIDE = 256
BLOCKS = DI // WIDE
MIB = 1024 * 1024
LIMIT = 62 * MIB
MESH_ID = pl.DeviceIdType.MESH
F32, BF16 = jnp.float32, jnp.bfloat16


def dot(a, b, dims=((1,), (0,))):
    return lax.dot_general(a, b, (dims, ((), ())), preferred_element_type=F32)


def exact_dot(a, b):
    return lax.dot_general(a, b, (((1,), (0,)), ((), ())), precision=lax.Precision.HIGHEST, preferred_element_type=F32)


def split(v):
    high = v.astype(BF16)
    return high, (v - high.astype(F32)).astype(BF16)


def dot3(a, b, dims=((1,), (0,))):
    (ah, al), (bh, bl) = a, b
    (ka,), (kb,) = dims
    return dot(jnp.concatenate([ah, al], axis=ka), jnp.concatenate([bh, bh], axis=kb), dims) + dot(ah, bl, dims)


def lane_iota(shape):
    return lax.broadcasted_iota(jnp.int32, shape, len(shape) - 1)


def row_iota(shape):
    return lax.broadcasted_iota(jnp.int32, shape, len(shape) - 2)


def head_spread():
    rows, lanes = row_iota((128, DI)), lane_iota((128, DI))
    hit = ((rows & 31) == (lanes >> 6)) & (rows < 96)
    return jnp.where(hit, 1.0, 0.0).astype(BF16)


def head_gather():
    rows, lanes = row_iota((DI, 128)), lane_iota((DI, 128))
    return jnp.where((rows >> 6) == lanes, 1.0, 0.0).astype(BF16)


def packed(v):
    v = jnp.where(lane_iota(v.shape) < H, v, 0.0)
    high = v.astype(BF16).astype(F32)
    rest = v - high
    middle = rest.astype(BF16).astype(F32)
    low = (rest - middle).astype(BF16).astype(F32)
    return (high + pltpu.roll(middle, 32, 1) + pltpu.roll(low, 64, 1)).astype(BF16)


def head_sums(v, gather):
    high, low = split(v)
    return dot(high, gather) + dot(low, gather)


def taps(xr_ref, start, lanes):
    rows = xr_ref[pl.ds(start, Q + HALO), lanes].astype(F32)
    count = Q + HALO
    return [pltpu.roll(rows, (count - (HALO - KCONV + 1) - k) % count, 0)[:Q] for k in range(KCONV)]


def conv_rows(xr_ref, kernel_ref, start, lanes):
    total = kernel_ref[KCONV : KCONV + 1, lanes]
    for k, rows in enumerate(taps(xr_ref, start, lanes)):
        total = total + kernel_ref[k : k + 1, lanes] * rows
    return total


def steps_of(raw, heads_ref):
    shifted = raw + heads_ref[0:1]
    dt = jnp.maximum(shifted, 0.0) + jnp.log1p(jnp.exp(-jnp.abs(shifted)))
    return jnp.where(lane_iota(raw.shape) < H, dt, 0.0), shifted


def rate_of(heads_ref):
    return -jnp.exp(heads_ref[1:2])


def causal():
    return row_iota((Q, Q)) >= lane_iota((Q, Q))


def whole(*shape):
    return pl.BlockSpec(shape, lambda i: (0,) * len(shape))


def once(*shape):
    return pl.BlockSpec(shape, lambda i: (0,) * len(shape), pipeline_mode=pl.Buffered(1))


def chunked(width, pick=lambda i: i):
    return pl.BlockSpec((Q, width), lambda i: (pick(i), 0))


def states_body(xr_ref, raw_ref, kernel_ref, heads_ref, xc_ref, dt_ref, cs_ref, local_ref, end_ref, decay_ref, spread, total):
    c = pl.program_id(0)
    start = pl.multiple_of(c * Q, Q)

    @pl.when(c == 0)
    def _():
        spread[...] = head_spread()
        end_ref[...] = jnp.zeros_like(end_ref)
        total[...] = jnp.zeros_like(total)

    lower = jnp.where(causal(), 1.0, 0.0)
    dt, _ = steps_of(raw_ref[...], heads_ref)
    cs = exact_dot(lower, dt * rate_of(heads_ref))
    last = cs[Q - 1 : Q]
    dt_ref[...] = dt
    cs_ref[...] = cs
    total[0:1] += last
    dt_pack, tail_pack = packed(dt), packed(jnp.exp(last - cs))
    keep_pack = packed(jnp.broadcast_to(jnp.exp(last), (16, 128)))
    both = slice(DI, CONV)
    mixed = conv_rows(xr_ref, kernel_ref, start, both)
    xc_ref[:, both] = mixed
    write = (mixed * jax.nn.sigmoid(mixed))[:, :N]
    write_t = split(write.T)
    for b in range(BLOCKS):
        lanes = slice(b * WIDE, (b + 1) * WIDE)
        conv = conv_rows(xr_ref, kernel_ref, start, lanes)
        xc_ref[:, lanes] = conv
        scaled = conv * jax.nn.sigmoid(conv) * dot(dt_pack, spread[:, lanes])
        tailed = scaled * dot(tail_pack, spread[:, lanes])
        keep = dot(keep_pack, spread[:, lanes])[0:1]
        before = end_ref[:, lanes]
        local_ref[:, lanes] = before
        end_ref[:, lanes] = keep * before + dot3(write_t, split(tailed))

    @pl.when(c == CHUNKS - 1)
    def _():
        keep_all = packed(jnp.broadcast_to(jnp.exp(total[0:1]), (16, 128)))
        decay_ref[...] = dot(keep_all, spread[...])[:8]


def chunk_states(xr, raw, kernel, heads):
    f = lambda *s: jax.ShapeDtypeStruct(s, F32)
    return pl.pallas_call(
        states_body,
        grid=(CHUNKS,),
        in_specs=[whole(TOK + HALO, CONV), chunked(128), whole(8, CONV), whole(8, 128)],
        out_specs=[chunked(CONV), chunked(128), chunked(128), chunked(DI), whole(N, DI), whole(8, DI)],
        out_shape=[f(TOK, CONV), f(TOK, 128), f(TOK, 128), f(CHUNKS * N, DI), f(N, DI), f(8, DI)],
        scratch_shapes=[pltpu.VMEM((128, DI), BF16), pltpu.VMEM((8, 128), F32)],
        compiler_params=pltpu.CompilerParams(vmem_limit_bytes=LIMIT),
        cost_estimate=pl.CostEstimate(flops=2 * 10**9, bytes_accessed=20 * 10**6, transcendentals=10**6),
        name="chunk_states",
    )(xr, raw, kernel, heads)


class HandOver:
    def __init__(self, backward, local_ref, decay_ref, joined, from_mate, from_far, mate_decay, send, recv):
        self.local, self.decay = local_ref, decay_ref
        self.from_mate, self.from_far, self.joined = from_mate, from_far, joined
        self.mate_decay, self.send, self.recv = mate_decay, send, recv
        rep, shard = lax.axis_index("rep"), lax.axis_index("shard")
        x_lo, core = lax.div(shard, 2), lax.rem(shard, 2)
        self.core = 1 - core if backward else core
        self.chip = 1 - x_lo if backward else x_lo
        self.sibling = {"rep": rep, "shard": x_lo * 2 + 1 - core}
        flip = (lambda k: 1 - k) if backward else (lambda k: k)
        self.other = [{"rep": rep, "shard": (1 - x_lo) * 2 + flip(k)} for k in range(2)]

    def greet(self):
        return [self.sibling] + self.other

    def copy(self, src, dst, k, target):
        return pltpu.make_async_remote_copy(
            src_ref=src, dst_ref=dst, send_sem=self.send.at[k], recv_sem=self.recv.at[k],
            device_id=target, device_id_type=MESH_ID,
        )

    def to_mate(self):
        return self.copy(self.local, self.from_mate, 0, self.sibling)

    def decay_to_mate(self):
        return self.copy(self.decay, self.mate_decay, 5, self.sibling)

    def across(self, k):
        rows = pl.ds(k * (N // 2), N // 2)
        return self.copy(self.joined.at[rows], self.from_far.at[rows], 1 + k, self.other[k])

    def swap(self, k):
        rows = pl.ds(k * (N // 2), N // 2)
        return self.copy(self.from_far.at[rows], self.from_far.at[rows], 3 + k, self.sibling)

    def begin(self):
        @pl.when(self.core == 0)
        def _():
            self.to_mate().start()
            self.decay_to_mate().start()

    def middle(self):
        @pl.when(self.core == 1)
        def _():
            self.to_mate().wait_recv()
            self.decay_to_mate().wait_recv()

        @pl.when((self.core == 1) & (self.chip == 0))
        def _():
            for b in range(BLOCKS):
                lanes = slice(b * WIDE, (b + 1) * WIDE)
                self.joined[:, lanes] = self.decay[0:1, lanes] * self.from_mate[:, lanes] + self.local[:, lanes]
            for k in range(2):
                self.across(k).start()

    def late(self):
        for k in range(2):
            @pl.when((self.chip == 1) & (self.core == k))
            def _():
                self.across(k).wait_recv()
                self.swap(k).start()

    def finish(self):
        for k in range(2):
            @pl.when((self.chip == 1) & (self.core == k))
            def _():
                self.swap(1 - k).wait_recv()
                self.swap(k).wait_send()

        @pl.when(self.core == 0)
        def _():
            self.to_mate().wait_send()
            self.decay_to_mate().wait_send()

        @pl.when((self.chip == 0) & (self.core == 1))
        def _():
            for k in range(2):
                self.across(k).wait_send()

        @pl.when((self.chip == 0) & (self.core == 0))
        def _():
            self.from_far[...] = jnp.zeros_like(self.from_far)

        @pl.when((self.chip == 0) & (self.core == 1))
        def _():
            self.from_far[...] = self.from_mate[...]

        @pl.when((self.chip == 1) & (self.core == 1))
        def _():
            for b in range(BLOCKS):
                lanes = slice(b * WIDE, (b + 1) * WIDE)
                self.from_far[:, lanes] = self.mate_decay[0:1, lanes] * self.from_far[:, lanes] + self.from_mate[:, lanes]


def greet_all(partners):
    barrier = pltpu.get_barrier_semaphore()
    for partner in partners:
        pl.semaphore_signal(barrier, inc=1, device_id=partner, device_id_type=MESH_ID)
    pl.semaphore_wait(barrier, len(partners))


HAND_SCRATCH = [
    pltpu.VMEM((N, DI), F32), pltpu.VMEM((N, DI), F32),
    pltpu.VMEM((8, DI), F32), pltpu.SemaphoreType.DMA((6,)), pltpu.SemaphoreType.DMA((6,)),
]


def side_by_side(high, first):
    zero = jnp.zeros_like(high)
    return jnp.concatenate([jnp.where(first, high, zero), jnp.where(first, zero, high)], axis=0)


def outputs_body(xc_ref, dt_ref, cs_ref, local_ref, end_ref, decay_ref, z_ref, heads_ref, gain_ref,
                 y_ref, state_ref, gated_ref, turned_ref, total_ref, spread, q_ref, inside, passed, joined, *hand):
    step = pl.program_id(0)
    c = lax.rem(step, CHUNKS)
    state_in = hand[1]
    over = HandOver(False, end_ref, decay_ref, joined, *hand)
    mixed = xc_ref[:, DI:CONV]
    mixed = mixed * jax.nn.sigmoid(mixed)
    read = split(mixed[:, N:])
    dt, cs = dt_ref[...], cs_ref[...]
    dt_pack = packed(dt)

    @pl.when(step == 0)
    def _():
        greet_all(over.greet())
        over.begin()
        spread[...] = head_spread()
        passed[...] = jnp.zeros_like(passed)

    @pl.when(step < CHUNKS)
    def _():
        below = causal()
        first = lane_iota((Q, 128)) < P_SIZE
        cs_t = cs.T
        cross = jnp.where(below, dot3(read, split(mixed[:, :N]), ((1,), (1,))), 0.0)
        for b in range(BLOCKS):
            lanes = slice(b * WIDE, (b + 1) * WIDE)
            conv = xc_ref[:, lanes]
            scaled_high, scaled_low = split(conv * jax.nn.sigmoid(conv) * dot(dt_pack, spread[:, lanes]))
            for half in range(2):
                factors = []
                for h in (4 * b + 2 * half, 4 * b + 2 * half + 1):
                    gap = jnp.where(below, cs[:, h : h + 1] - cs_t[h : h + 1, :], 0.0)
                    factors.append(jnp.exp(gap) * cross)
                high, low = split(jnp.concatenate(factors, axis=1))
                at = slice(half * 128, (half + 1) * 128)
                right = side_by_side(scaled_high[:, at], first)
                right_low = side_by_side(scaled_low[:, at], first)
                doubled = dot(high, jnp.concatenate([right, right_low], axis=1))
                place = slice(b * WIDE + half * 128, b * WIDE + (half + 1) * 128)
                inside[c, :, place] = doubled[:, :128] + doubled[:, 128:] + dot(low, right)

    @pl.when(step == 0)
    def _():
        over.middle()

    @pl.when(step == 2)
    def _():
        over.late()

    @pl.when(step == CHUNKS)
    def _():
        over.finish()

    @pl.when(step >= CHUNKS)
    def _():
        now_pack = packed(jnp.exp(cs))
        before_pack = packed(jnp.broadcast_to(jnp.exp(passed[0:1]), (16, 128)))
        skip_pack = packed(jnp.broadcast_to(heads_ref[2:3], (16, 128)))
        squares = jnp.zeros((Q, 1), F32)
        for b in range(BLOCKS):
            lanes = slice(b * WIDE, (b + 1) * WIDE)
            conv = xc_ref[:, lanes]
            inner = conv * jax.nn.sigmoid(conv)
            state = local_ref[:, lanes] + dot(before_pack, spread[:, lanes])[0:1] * state_in[:, lanes]
            state_ref[:, lanes] = state
            carried = dot(now_pack, spread[:, lanes]) * dot3(read, split(state))
            y = inside[c, :, lanes] + carried + dot(skip_pack, spread[:, lanes])[0:1] * inner
            y_ref[:, lanes] = y
            z = z_ref[:, lanes]
            q = y * (z * jax.nn.sigmoid(z))
            q_ref[:, lanes] = q
            squares = squares + jnp.sum(q * q, axis=1, keepdims=True)
        scale = lax.rsqrt(squares * (1.0 / DI) + NORM_EPS)
        for b in range(BLOCKS):
            lanes = slice(b * WIDE, (b + 1) * WIDE)
            gated = q_ref[:, lanes] * scale * gain_ref[0:1, lanes]
            gated_ref[:, lanes] = gated.astype(BF16)
            turned_ref[lanes, :] = gated.T.astype(BF16)
        passed[0:1] += cs[Q - 1 : Q]

    @pl.when(step == 2 * CHUNKS - 1)
    def _():
        for b in range(BLOCKS):
            lanes = slice(b * WIDE, (b + 1) * WIDE)
            total_ref[:, lanes] = end_ref[:, lanes] + decay_ref[0:1, lanes] * state_in[:, lanes]


def outputs(xc, dt, cs, local, end, decay, z, heads, gain):
    f = lambda *s: jax.ShapeDtypeStruct(s, F32)
    both = lambda i: lax.rem(i, CHUNKS)
    late = lambda i: jnp.maximum(i - CHUNKS, 0)
    return pl.pallas_call(
        outputs_body,
        grid=(2 * CHUNKS,),
        in_specs=[
            chunked(CONV, both), chunked(128, both), chunked(128, both), chunked(DI, late), whole(N, DI), whole(8, DI),
            chunked(DI, late), whole(8, 128), whole(1, DI),
        ],
        out_specs=[
            chunked(DI, late), chunked(DI, late), chunked(DI, late), pl.BlockSpec((DI, Q), lambda i: (0, late(i))), whole(N, DI),
        ],
        out_shape=[
            f(TOK, DI), f(CHUNKS * N, DI), jax.ShapeDtypeStruct((TOK, DI), BF16), jax.ShapeDtypeStruct((DI, TOK), BF16), f(N, DI),
        ],
        scratch_shapes=[
            pltpu.VMEM((128, DI), BF16), pltpu.VMEM((Q, DI), F32), pltpu.VMEM((CHUNKS, Q, DI), F32), pltpu.VMEM((8, 128), F32),
            pltpu.VMEM((N, DI), F32), *HAND_SCRATCH,
        ],
        compiler_params=pltpu.CompilerParams(collective_id=2, has_side_effects=True, vmem_limit_bytes=LIMIT),
        cost_estimate=pl.CostEstimate(flops=5 * 10**9, bytes_accessed=30 * 10**6, transcendentals=3 * 10**6),
        name="outputs",
    )(xc, dt, cs, local, end, decay, z, heads, gain)


def gate_back_body(dgated_ref, y_ref, z_ref, mixed_ref, cs_ref, gain_ref, gated_turned, turned, cot,
                   dys_ref, dz_ref, own_ref, start_ref, dgain_ref, mate_gated, mate_turned, mate_cot, spread, send, recv):
    rep, shard = lax.axis_index("rep"), lax.axis_index("shard")
    core = lax.rem(shard, 2)
    sibling = {"rep": rep, "shard": shard + 1 - 2 * core}

    def factors():
        pairs = [(cot, mate_cot)]
        for source, target, size in ((gated_turned, mate_gated, 512), (turned, mate_turned, 256)):
            for x_lo in range(2):
                rows = pl.ds(pl.multiple_of((x_lo * 2 + 1 - core) * size, size), size)
                pairs.append((source.at[rows], target.at[pl.ds(x_lo * size, size)]))
        return [
            pltpu.make_async_remote_copy(
                src_ref=a, dst_ref=b, send_sem=send.at[k], recv_sem=recv.at[k], device_id=sibling, device_id_type=MESH_ID
            )
            for k, (a, b) in enumerate(pairs)
        ]

    @pl.when(pl.program_id(0) == 0)
    def _():
        greet_all([sibling])
        for copy in factors():
            copy.start()
        spread[...] = head_spread()
        dgain_ref[...] = jnp.zeros_like(dgain_ref)
        start_ref[...] = jnp.zeros_like(start_ref)

    cs = cs_ref[...]
    squares = jnp.zeros((Q, 1), F32)
    crossed = jnp.zeros((Q, 1), F32)
    for b in range(BLOCKS):
        lanes = slice(b * WIDE, (b + 1) * WIDE)
        z = z_ref[:, lanes]
        q = y_ref[:, lanes] * (z * jax.nn.sigmoid(z))
        dn = dgated_ref[:, lanes] * gain_ref[0:1, lanes]
        squares = squares + jnp.sum(q * q, axis=1, keepdims=True)
        crossed = crossed + jnp.sum(dn * q, axis=1, keepdims=True)
    scale = lax.rsqrt(squares * (1.0 / DI) + NORM_EPS)
    pull = crossed * (1.0 / DI) * scale * scale * scale
    mixed = mixed_ref[:, N:]
    read_t = split((mixed * jax.nn.sigmoid(mixed)).T)
    now_pack = packed(jnp.exp(cs))
    keep_pack = packed(jnp.broadcast_to(jnp.exp(cs[Q - 1 : Q]), (16, 128)))
    for b in range(BLOCKS):
        lanes = slice(b * WIDE, (b + 1) * WIDE)
        z = z_ref[:, lanes]
        gate = jax.nn.sigmoid(z)
        open_ = z * gate
        y = y_ref[:, lanes]
        q = y * open_
        dgated = dgated_ref[:, lanes]
        dgain_ref[0:1, lanes] += jnp.sum(dgated * q * scale, axis=0, keepdims=True)
        dq = scale * (dgated * gain_ref[0:1, lanes]) - q * pull
        dys = dq * open_
        dys_ref[:, lanes] = dys
        dz_ref[:, lanes] = (dq * y * (gate + open_ * (1.0 - gate))).astype(BF16)
        early = dys * dot(now_pack, spread[:, lanes])
        own = dot3(read_t, split(early))
        own_ref[:, lanes] = own
        start_ref[:, lanes] = dot(keep_pack, spread[:, lanes])[0:1] * start_ref[:, lanes] + own

    @pl.when(pl.program_id(0) == CHUNKS - 1)
    def _():
        for copy in factors():
            copy.wait()


def gate_back(dgated, y, z, xc, cs, gain, gated_turned, turned, cot):
    f = lambda *s: jax.ShapeDtypeStruct(s, F32)
    turn = lambda i: CHUNKS - 1 - i
    hbm = pl.BlockSpec(memory_space=pl.ANY)
    return pl.pallas_call(
        gate_back_body,
        grid=(CHUNKS,),
        in_specs=[
            chunked(DI, turn), chunked(DI, turn), chunked(DI, turn),
            pl.BlockSpec((Q, WIDE), lambda i: (turn(i), DI // WIDE)), chunked(128, turn), whole(1, DI), *[hbm] * 3,
        ],
        out_specs=[chunked(DI, turn), chunked(DI, turn), chunked(DI, turn), whole(N, DI), whole(8, DI), *[hbm] * 3],
        out_shape=[
            f(TOK, DI), jax.ShapeDtypeStruct((TOK, DI), BF16), f(CHUNKS * N, DI), f(N, DI), f(8, DI),
            *[jax.ShapeDtypeStruct(shape, BF16) for shape in ((DI // 2, TOK), (D // 2, TOK), (TOK, D))],
        ],
        scratch_shapes=[pltpu.VMEM((128, DI), BF16), pltpu.SemaphoreType.DMA((5,)), pltpu.SemaphoreType.DMA((5,))],
        compiler_params=pltpu.CompilerParams(collective_id=5, has_side_effects=True, vmem_limit_bytes=LIMIT),
        cost_estimate=pl.CostEstimate(flops=2 * 10**9, bytes_accessed=30 * 10**6, transcendentals=2 * 10**6),
        name="gate_back",
    )(dgated, y, z, xc, cs, gain, gated_turned, turned, cot)


def my_place():
    rep, shard = lax.axis_index("rep"), lax.axis_index("shard")
    return {
        "x": lax.rem(lax.div(rep, 4), 2) * 2 + lax.div(shard, 2),
        "y": lax.div(rep, 8),
        "z": lax.rem(rep, 4),
        "core": lax.rem(shard, 2),
    }


def device_at(place):
    rep = place["y"] * 8 + lax.div(place["x"], 2) * 4 + place["z"]
    return {"rep": rep, "shard": lax.rem(place["x"], 2) * 2 + place["core"]}


def moved(place, axis, by):
    return {**place, axis: lax.rem(place[axis] + by, 4)}


def remote(src, dst, send, recv, target):
    return pltpu.make_async_remote_copy(
        src_ref=src, dst_ref=dst, send_sem=send, recv_sem=recv, device_id=target, device_id_type=MESH_ID
    )


def halves(ref, length):
    return ref.at[pl.ds(0, length // 2)], ref.at[pl.ds(length // 2, length // 2)]


def add_to(dst, sources):
    shape = dst.shape

    def one(at):
        value = dst[at]
        for source in sources:
            value = value + source[at]
        dst[at] = value

    if len(shape) == 4:
        def body(i, carry):
            for k in range(shape[1]):
                one((i, k))
            return carry

        lax.fori_loop(0, shape[0], body, 0)
    elif len(shape) == 3:
        for k in range(shape[0]):
            one((k,))
    else:
        one((Ellipsis,))


def kept_shape(order, rows):
    return tuple(2 if axis == "x" else 4 for axis in order) + (rows, 128)


def sums_scratch(orders, rows, items):
    f = lambda *s: pltpu.VMEM(s + (128,), F32)
    scratch = []
    for r in rows:
        half = [f(2, 4, r), f(2, r), f(r // 2)]
        full = [f(4, 4, r), f(4, r), f(r)]
        scratch += [f(4, 4, 4, r), *half, *full, *half, *full]
    dma = pltpu.SemaphoreType.DMA
    count = len(rows)
    return scratch + [
        dma((count, 3, 6)), dma((count, 3, 6)),
        dma((count + len(items), 8)), dma((count + len(items), 8)), dma((count,)),
    ]


class Sums:
    def __init__(self, orders, rows, items, outs, scratch):
        self.orders, self.rows, self.items, self.outs = orders, rows, items, outs
        self.data, self.low_half, self.from_left, self.high_half, self.from_right = [], [], [], [], []
        for t in range(len(rows)):
            part = scratch[t * 13 : (t + 1) * 13]
            self.data.append(part[0])
            self.low_half.append(part[1:4])
            self.from_left.append(part[4:7])
            self.high_half.append(part[7:10])
            self.from_right.append(part[10:13])
        self.ring_send, self.ring_recv, self.gather_send, self.gather_recv, self.keep_sem = scratch[13 * len(rows) :]
        self.here = here = my_place()
        self.core = here["core"]
        self.place = {"x": lax.div(here["x"], 2), "y": here["y"], "z": here["z"]}
        self.sibling = device_at({**here, "core": 1 - here["core"]})
        self.across = device_at(moved(here, "x", 2))
        self.right = {a: device_at(moved(here, a, 1)) for a in "xyz"}
        self.left = {a: device_at(moved(here, a, 3)) for a in "xyz"}
        self.pending = []

    def greet(self):
        return [self.sibling, self.across] + [self.right[a] for a in "xyz"] + [self.left[a] for a in "xyz"]

    def slot(self, axis, by):
        return lax.rem(self.here[axis] + by, 4)

    def at(self, t, step):
        return self.slot(self.orders[t][0], step)

    def go(self, make):
        make().start()
        self.pending.append(make)


    def level(self, t, stage):
        return self.data[t] if stage == 0 else self.from_left[t][stage - 1]

    def length(self, t, stage):
        return (4, 4, self.rows[t])[stage]

    def ring(self, t, stage, name):
        axis, length = self.orders[t][stage], self.length(t, stage)
        send, recv = self.ring_send.at[t, stage], self.ring_recv.at[t, stage]
        now = self.level(t, stage)
        right, left = self.right[axis], self.left[axis]
        got_left_low, got_left_high = halves(self.from_left[t][stage], length)
        got_right_low, got_right_high = halves(self.from_right[t][stage], length)
        if name == "far_right":
            return remote(halves(now.at[self.slot(axis, 2)], length)[0], self.low_half[t][stage], send.at[0], recv.at[0], right)
        if name == "far_left":
            return remote(halves(now.at[self.slot(axis, 2)], length)[1], self.high_half[t][stage], send.at[1], recv.at[1], left)
        if name == "near_right":
            return remote(halves(now.at[self.slot(axis, 1)], length)[1], got_left_high, send.at[2], recv.at[2], right)
        if name == "near_left":
            return remote(halves(now.at[self.slot(axis, 3)], length)[0], got_right_low, send.at[3], recv.at[3], left)
        if name == "last_right":
            return remote(halves(now.at[self.slot(axis, 1)], length)[0], got_left_low, send.at[4], recv.at[4], right)
        return remote(halves(now.at[self.slot(axis, 3)], length)[1], got_right_high, send.at[5], recv.at[5], left)

    def ring_go(self, t, stage, *names):
        for name in names:
            self.go(functools.partial(self.ring, t, stage, name))

    def relay(self, t, stage):
        axis, length, now = self.orders[t][stage], self.length(t, stage), self.level(t, stage)
        self.ring(t, stage, "far_right").wait_recv()
        add_to(halves(now.at[self.slot(axis, 1)], length)[0], [self.low_half[t][stage]])
        self.ring_go(t, stage, "last_right")
        self.ring(t, stage, "far_left").wait_recv()
        add_to(halves(now.at[self.slot(axis, 3)], length)[1], [self.high_half[t][stage]])
        self.ring_go(t, stage, "last_left")

    def settle(self, t, stage):
        for name in ("near_right", "near_left", "last_right", "last_left"):
            self.ring(t, stage, name).wait_recv()
        mine = self.level(t, stage).at[self.slot(self.orders[t][stage], 0)]
        add_to(self.from_left[t][stage], [mine, self.from_right[t][stage]])
        if stage < 2:
            self.ring_go(t, stage + 1, "far_right", "far_left", "near_right", "near_left")


    def piece(self, t, x_hi):
        place = {**self.place, "x": x_hi}
        return self.outs[t].at[tuple(place[a] for a in self.orders[t])]

    def keep(self, t):
        return pltpu.make_async_copy(self.from_left[t][2], self.piece(t, self.place["x"]), self.keep_sem.at[t])

    def pair(self, t, x_hi):
        return remote(self.from_left[t][2], self.piece(t, x_hi), self.gather_send.at[t, 0], self.gather_recv.at[t, 0], self.across)

    def share(self, t):
        self.settle(t, 2)
        self.keep(t).start()
        self.go(functools.partial(self.pair, t, self.place["x"]))

    def region(self, item, stage, by, half):
        t, first, count, order = self.items[item]
        at = {"y": pl.ds(self.here["y"], 1), "z": pl.ds(self.here["z"], 1), "x": pl.ds(0, 2) if half is None else pl.ds(half, 1)}
        if stage == 1:
            at[order[0]] = pl.ds(0, 4)
        at[order[stage]] = pl.ds(self.slot(order[stage], by), 1)
        return self.outs[t].at[tuple(at[a] for a in self.orders[t]) + (pl.ds(first, count),)]

    def spread_copy(self, item, stage, k, arriving=False):
        axis = self.items[item][3][stage]
        if arriving:
            piece = self.region(item, stage, *((3, None), (1, None), (2, 0), (2, 1))[k])
        else:
            piece = self.region(item, stage, *((0, None), (0, None), (3, 0), (1, 1))[k])
        target = (self.left if k % 2 else self.right)[axis]
        row = len(self.rows) + item
        return remote(piece, piece, self.gather_send.at[row, 4 * stage + k], self.gather_recv.at[row, 4 * stage + k], target)

    def items_of(self, t):
        return [i for i, item in enumerate(self.items) if item[0] == t]

    def arrival(self, item, stage, k):
        self.spread_copy(item, stage, k, arriving=True).wait_recv()

    def paired(self, t):
        self.keep(t).wait()
        self.pair(t, 1 - self.place["x"]).wait_recv()

    def arrive(self, t):
        for item in self.items_of(t):
            self.arrival(item, 0, 2)
            self.arrival(item, 0, 3)

    def spread_out(self, t, stage):
        for item in self.items_of(t):
            for k in range(2):
                self.go(functools.partial(self.spread_copy, item, stage, k))

    def spread_on(self, t, stage):
        for item in self.items_of(t):
            for k in range(2):
                self.arrival(item, stage, k)
                self.go(functools.partial(self.spread_copy, item, stage, 2 + k))

    def spread_end(self, t):
        for item in self.items_of(t):
            self.arrival(item, 1, 2)
            self.arrival(item, 1, 3)

    def close(self):
        for make in self.pending:
            make().wait_send()


def kept_rows(turned, core):
    return jnp.concatenate([turned[pl.ds(pl.multiple_of((x_lo * 2 + core) * 256, 256), 256), :] for x_lo in range(2)], axis=0)


def gate_block(sums, own, mate, step):
    at = sums.slot("z", step)
    lanes = pl.ds(pl.multiple_of(at * 512, 512), 512)
    product = dot(kept_rows(own[0], sums.core), own[1][:, lanes]) + dot(mate[0][...], mate[1][:, lanes])
    tall, short = sums.data[0], sums.data[2]
    for x_lo in range(2):
        for hi in range(2):
            first, x = x_lo * 256 + hi * 128, hi * 2 + x_lo
            for y in range(4):
                columns = slice(y * 128, (y + 1) * 128)
                tall[at, x, y] = product[first : first + TALL, columns]
                short[y, at, x] = product[first + TALL : first + 128, columns]
    sums.ring_go(0, 0, *SENDS[step])


def out_block(sums, own, mate, step):
    at = sums.slot("x", step)
    x_lo, x_hi = lax.rem(at, 2), lax.div(at, 2)
    rows = pl.ds(pl.multiple_of((x_lo * 2 + sums.core) * 512, 512), 512)
    lanes = pl.ds(pl.multiple_of(x_hi * 512, 512), 512)
    product = dot(own[0][rows, :], own[1][:, lanes])
    product = product + dot(mate[0][pl.ds(pl.multiple_of(x_lo * 512, 512), 512), :], mate[1][:, lanes])
    tall, short = sums.data[1], sums.data[3]
    for y in range(4):
        columns = slice(y * 128, (y + 1) * 128)
        for z in range(4):
            tall[at, y, z] = product[z * 128 : z * 128 + TALL, columns]
            short[y, z, at] = product[z * 128 + TALL : (z + 1) * 128, columns]
    sums.ring_go(1, 0, *SENDS[step])


SENDS = {2: ("far_right", "far_left"), 1: ("near_right",), 3: ("near_left",), 0: ()}
SPAN = 768


def stretches(piece, band):
    at, end = 48 * piece, 48 * piece + 48
    while at < end:
        count = min(band - at % band, end - at)
        yield at - 48 * piece, count, at // band, at % band
        at += count


def inner_block(which, steps, core, own, mate, at, store):
    lanes = slice(which * SPAN, (which + 1) * SPAN)
    if which == 0:
        x_lo, half = lax.rem(at, 2), lax.div(at, 2) * 128
        rows = pl.ds(pl.multiple_of((x_lo * 2 + core) * 256 + half, 128), 128)
        product = dot(own[0][rows, :], own[1][:, lanes])
        product = product + dot(mate[0][pl.ds(pl.multiple_of(x_lo * 256 + half, 128), 128), :], mate[1][:, lanes])
        for piece in range(16):
            for row, count, tile, start in stretches(piece, 128):
                store(piece // 4, piece % 4, pl.ds(row, count), product[start : start + count, tile * 128 : (tile + 1) * 128])
            first = pl.multiple_of(x_lo * 256 + half + piece * 8, 8)
            store(piece // 4, piece % 4, pl.ds(48, 8), steps[pl.ds(first, 8)])
            store(piece // 4, piece % 4, pl.ds(56, 8), jnp.zeros((8, 128), F32))
        return

    def bands(ref, first):
        parts = [ref[pl.ds(pl.multiple_of(first(x_lo) + at * 64, 64), 64), :] for x_lo in range(2)]
        return jnp.concatenate(parts, axis=0)

    product = dot(bands(own[0], lambda x_lo: (x_lo * 2 + core) * 256), own[1][:, lanes])
    product = product + dot(bands(mate[0], lambda x_lo: x_lo * 256), mate[1][:, lanes])
    for x_lo in range(2):
        for piece in range(8):
            i, k = (piece // 2, piece % 2 * 2 + x_lo) if which == 1 else (piece // 4 * 2 + x_lo, piece % 4)
            for row, count, tile, start in stretches(piece, 64):
                start += x_lo * 64
                store(i, k, pl.ds(row, count), product[start : start + count, tile * 128 : (tile + 1) * 128])


def make_block(sums, t, maker, own, mate, step):
    at = sums.at(t, step)

    def store(i, k, rows, tile):
        sums.data[t][at, i, k, rows] = tile

    maker(sums.core, own, mate, at, store)
    sums.ring_go(t, 0, *SENDS[step])


TALL, SHORT = 96, 32
EARLY = (
    ("zxy", "xyz", "yzx", "yzx"), (TALL, TALL, SHORT, SHORT),
    ((0, 0, TALL, "zy"), (1, 0, TALL, "yz"), (2, 0, SHORT, "yz"), (3, 0, SHORT, "zy")),
)
LATE = (("xyz", "yzx", "zxy"), (64, 48, 48), ((0, 0, 32, "yz"), (0, 32, 32, "zy"), (1, 0, 48, "zy"), (2, 0, 48, "yz")))


def spread_scratch(items):
    dma = pltpu.SemaphoreType.DMA
    return [dma((len(items), 8)), dma((len(items), 8))]


class Spread(Sums):
    def __init__(self, orders, rows, items, outs, scratch):
        self.orders, self.rows, self.items, self.outs = orders, (), items, outs
        self.gather_send, self.gather_recv = scratch
        self.here = my_place()
        self.right = {a: device_at(moved(self.here, a, 1)) for a in "xyz"}
        self.left = {a: device_at(moved(self.here, a, 3)) for a in "xyz"}
        self.pending = []


def core_back_body(xc_ref, xr_ref, raw_ref, dt_ref, cs_ref, cs_all, state_ref, next_ref, total_ref, y_ref, dys_ref, own_ref, start_ref,
                   decay_ref, heads_ref, kernel_ref, turned_far, gated_far, cot_far, dz_far, mate_turned_far, mate_gated_far, mate_cot_far,
                   dxr_ref, draw_ref, dkernel_ref, dheads_ref, sum0, sum1, sum2, sum3, far_dxr, far_draw,
                   turned_ref, gated_ref, cot_ref, dz_ref, mate_turned, mate_gated, mate_cot, load_sem,
                   mate_dz, dxr_send, draw_send, pass_send, pass_recv, own_sem, spread, gather, dstate, inside, dmixed_ref, dxc, edge_out, edge_in, follow, edge_send, edge_recv, *others):
    step = pl.program_id(0)
    c = lax.rem(step, CHUNKS)
    hand, sums_part = others[:5], others[5:]
    over = HandOver(True, start_ref, decay_ref, dstate.at[CHUNKS - 1], *hand)
    sums = Sums(*EARLY, (sum0, sum1, sum2, sum3), sums_part)

    def pass_on(k):
        if k < 4:
            lanes = pl.ds(pl.multiple_of(sums.slot("z", k) * 512, 512), 512)
            source, target = dz_far.at[:, lanes], mate_dz.at[:, lanes]
        elif k < 8:
            source, target = dxr_send.at[k % 2], far_dxr.at[pl.ds((k - 4) * Q, Q)]
        else:
            source, target = draw_send, far_draw
        return remote(source, target, pass_send.at[k], pass_recv.at[k], sums.sibling)

    owns = [
        pltpu.make_async_copy(own_ref.at[pl.ds((k + 1) * N, N)], dstate.at[k], own_sem.at[k]) for k in range(CHUNKS - 1)
    ]
    loads = [
        pltpu.make_async_copy(far, near, load_sem.at[k])
        for k, (far, near) in enumerate((
            (gated_far, gated_ref), (cot_far, cot_ref), (mate_gated_far, mate_gated), (mate_cot_far, mate_cot),
            (dz_far, dz_ref), (turned_far, turned_ref), (mate_turned_far, mate_turned),
        ))
    ]
    plan = core_plan(
        sums, loads, pass_on, (turned_ref, dz_ref), (mate_turned, mate_dz), (gated_ref, cot_ref), (mate_gated, mate_cot)
    )

    def act(first, count, b):
        for s in range(first, first + count):
            actions = plan.get((s, b))
            if actions:
                @pl.when(step == s)
                def _():
                    for action in actions:
                        action()

    rep, shard = lax.axis_index("rep"), lax.axis_index("shard")
    before = {"rep": rep, "shard": lax.rem(shard + 3, 4)}
    after = {"rep": rep, "shard": lax.rem(shard + 1, 4)}
    edge = pltpu.make_async_remote_copy(
        src_ref=edge_out, dst_ref=edge_in, send_sem=edge_send, recv_sem=edge_recv, device_id=before, device_id_type=MESH_ID
    )
    above = row_iota((Q, Q)) <= lane_iota((Q, Q))
    dt, cs = dt_ref[...], cs_ref[...]
    last = cs[Q - 1 : Q]
    raw_mixed = xc_ref[:, DI:CONV]
    mixed_gate = jax.nn.sigmoid(raw_mixed)
    mixed = raw_mixed * mixed_gate
    write, read = split(mixed[:, :N]), split(mixed[:, N:])
    dt_pack, now_pack = packed(dt), packed(jnp.exp(cs))

    @pl.when(step == 0)
    def _():
        for load in loads:
            load.start()
        greet_all(sums.greet() + [{"rep": rep, "shard": 3 - shard}])
        over.begin()
        for k in (2, 1, 3, 0):
            pass_on(k).start()
        for own in owns:
            own.start()
        spread[...] = head_spread()
        gather[...] = head_gather()
        dkernel_ref[...] = jnp.zeros_like(dkernel_ref)
        dheads_ref[...] = jnp.zeros_like(dheads_ref)

    @pl.when(step < CHUNKS)
    def _():
        first = lane_iota((Q, 128)) < P_SIZE
        cs_t = cs.T
        cross_t = jnp.where(above, dot3(write, read, ((1,), (1,))), 0.0)
        dcross_t = jnp.zeros((Q, Q), F32)
        dread = jnp.zeros((Q, N), F32)
        for b in range(BLOCKS):
            lanes = slice(b * WIDE, (b + 1) * WIDE)
            conv = xc_ref[:, lanes]
            scaled_high, scaled_low = split(conv * jax.nn.sigmoid(conv) * dot(dt_pack, spread[:, lanes]))
            dys = dys_ref[:, lanes]
            dys_high, dys_low = split(dys)
            for half in range(2):
                at = slice(half * 128, (half + 1) * 128)
                sh, sl = scaled_high[:, at], scaled_low[:, at]
                right, right_low = side_by_side(dys_high[:, at], first), side_by_side(dys_low[:, at], first)
                dfactor = dot(jnp.concatenate([sh, sl], axis=1), jnp.concatenate([right, right], axis=1), ((1,), (1,)))
                dfactor = dfactor + dot(sh, right_low, ((1,), (1,)))
                factors = []
                for k in range(2):
                    h = 4 * b + 2 * half + k
                    fall = jnp.exp(jnp.where(above, cs_t[h : h + 1, :] - cs[:, h : h + 1], 0.0))
                    dcross_t = dcross_t + fall * dfactor[:, k * Q : (k + 1) * Q]
                    factors.append(fall * cross_t)
                high, low = split(jnp.concatenate(factors, axis=1))
                doubled = dot(high, jnp.concatenate([right, right_low], axis=1))
                place = slice(b * WIDE + half * 128, b * WIDE + (half + 1) * 128)
                inside[c, :, place] = doubled[:, :128] + doubled[:, 128:] + dot(low, right)
            dread = dread + dot3(split(dys * dot(now_pack, spread[:, lanes])), split(state_ref[:, lanes]), ((1,), (1,)))
            act(0, CHUNKS, b)
        dcross_t = jnp.where(above, dcross_t, 0.0)
        dmixed_ref[c, :, :N] = dot3(split(dcross_t), read)
        dmixed_ref[c, :, N:] = dread + dot3(split(dcross_t.T), write)

    @pl.when(step == 0)
    def _():
        over.middle()

    @pl.when(step == 2)
    def _():
        over.late()

    @pl.when(step == CHUNKS)
    def _():
        over.finish()
        later = hand[1]
        for b in range(BLOCKS):
            lanes = slice(b * WIDE, (b + 1) * WIDE)
            now = later[:, lanes]
            dstate[CHUNKS - 1, :, lanes] = now
            for k in range(CHUNKS - 2, -1, -1):
                if b == 0:
                    owns[k].wait()
                ends = jnp.broadcast_to(cs_all[(k + 2) * Q - 1 : (k + 2) * Q], (16, 128))
                now = dot(packed(jnp.exp(ends)), spread[:, lanes])[0:1] * now + dstate[k, :, lanes]
                dstate[k, :, lanes] = now

    @pl.when((step >= CHUNKS) & (step < 2 * CHUNKS))
    def _():
        rate = rate_of(heads_ref)
        upper = jnp.where(above, 1.0, 0.0)
        tail_pack = packed(jnp.exp(last - cs))
        skip_pack = packed(jnp.broadcast_to(heads_ref[2:3], (16, 128)))
        dwrite = dmixed_ref[c, :, :N]
        dstep = jnp.zeros((Q, 128), F32)
        dcs = jnp.zeros((Q, 128), F32)
        dskip = jnp.zeros((1, 128), F32)
        final = c == CHUNKS - 1
        here = lax.rem(c, 2)
        for b in range(BLOCKS):
            lanes = slice(b * WIDE, (b + 1) * WIDE)
            conv = xc_ref[:, lanes]
            gate = jax.nn.sigmoid(conv)
            inner = conv * gate
            dt_wide = dot(dt_pack, spread[:, lanes])
            tail_wide = dot(tail_pack, spread[:, lanes])
            scaled = inner * dt_wide
            dys = dys_ref[:, lanes]
            later = dstate[c, :, lanes]
            later_split = split(later)
            dscaled = inside[c, :, lanes] + tail_wide * dot3(write, later_split)
            dwrite = dwrite + dot3(split(scaled * tail_wide), later_split, ((1,), (1,)))
            skip_wide = dot(skip_pack, spread[:, lanes])[0:1]
            dinner = dscaled * dt_wide + skip_wide * dys
            dxc[here, :, lanes] = dinner * (gate + inner * (1.0 - gate))
            some = gather[b * WIDE : (b + 1) * WIDE]
            dstep = dstep + head_sums(dscaled * inner, some)
            dcs = dcs + head_sums(dys * (y_ref[:, lanes] - skip_wide * inner) - scaled * dscaled, some)
            ahead = jnp.where(final, total_ref[:, lanes], next_ref[:, lanes])
            linked = jnp.sum(later * ahead, axis=0, keepdims=True)
            skipped = jnp.sum(dys * inner, axis=0, keepdims=True)
            heads_sum = head_sums(jnp.concatenate([jnp.broadcast_to(linked, (8, WIDE)), jnp.broadcast_to(skipped, (8, WIDE))], axis=0), some)
            dcs = dcs + jnp.where(row_iota((Q, 128)) == Q - 1, heads_sum[0:1], 0.0)
            dskip = dskip + heads_sum[8:9]
            act(CHUNKS, CHUNKS, b)
        dmixed = jnp.concatenate([dwrite, dmixed_ref[c, :, N:]], axis=1)
        dxc[here, :, DI:CONV] = dmixed * (mixed_gate + mixed * (1.0 - mixed_gate))
        dld = exact_dot(upper, dcs)
        _, shifted_raw = steps_of(raw_ref[...], heads_ref)
        draw = (dstep + dld * rate) * jax.nn.sigmoid(shifted_raw)
        draw = jnp.where(lane_iota(draw.shape) < H, draw, 0.0)
        draw_ref[...] = draw.astype(BF16)
        draw_send[pl.ds(pl.multiple_of(c * Q, Q), Q), :] = draw.astype(BF16)
        dheads_ref[0:1] += jnp.sum(draw, axis=0, keepdims=True)
        dheads_ref[1:2] += jnp.sum(dld * dt, axis=0, keepdims=True) * rate
        dheads_ref[2:3] += dskip

    @pl.when(step == 2 * CHUNKS - 1)
    def _():
        pass_on(8).start()

    @pl.when(step == CHUNKS)
    def _():
        edge_out[...] = dxc[0, 0:8]

        @pl.when(shard > 0)
        def _():
            edge.start()

    @pl.when(step == 2 * CHUNKS)
    def _():
        @pl.when(shard < 3)
        def _():
            edge.wait_recv()

        @pl.when(shard == 3)
        def _():
            edge_in[...] = jnp.zeros_like(edge_in)

        @pl.when(shard > 0)
        def _():
            edge.wait_send()

    @pl.when(step > CHUNKS)
    def _():
        done = step - CHUNKS - 1
        there = lax.rem(done, 2)
        start = pl.multiple_of(done * Q, Q)

        @pl.when(step == 2 * CHUNKS)
        def _():
            follow[...] = edge_in[...]

        @pl.when(step < 2 * CHUNKS)
        def _():
            follow[...] = dxc[1 - there, 0:8]

        for k in (2, 3):
            @pl.when(done == k)
            def _():
                pass_on(4 + k - 2).wait_send()

        for b in range(CONV // WIDE):
            lanes = slice(b * WIDE, (b + 1) * WIDE)
            now = dxc[there, :, lanes]
            rows = jnp.concatenate([now, follow[:, lanes]], axis=0)
            total = kernel_ref[KCONV - 1 : KCONV, lanes] * now
            for k in range(KCONV - 1):
                forward = KCONV - 1 - k
                total = total + kernel_ref[k : k + 1, lanes] * pltpu.roll(rows, Q + 8 - forward, 0)[:Q]
            dxr_ref[:, lanes] = total.astype(BF16)
            dxr_send[there, :, lanes] = total.astype(BF16)
            for k, seen in enumerate(taps(xr_ref, start, lanes)):
                dkernel_ref[k : k + 1, lanes] += jnp.sum(now * seen, axis=0, keepdims=True)
            dkernel_ref[KCONV : KCONV + 1, lanes] += jnp.sum(now, axis=0, keepdims=True)
            act(2 * CHUNKS, 1, b)

        for k in range(CHUNKS):
            @pl.when(done == k)
            def _():
                pass_on(4 + k).start()

    @pl.when(step == 2 * CHUNKS)
    def _():
        for t in range(4):
            sums.arrive(t)
        sums.close()
        for k in range(4, 9):
            pass_on(k).wait_recv()
        for k in (0, 1, 2, 3, 6, 7, 8):
            pass_on(k).wait_send()


def core_plan(sums, loads, pass_on, gate_own, gate_mate, out_own, out_mate):
    part = functools.partial
    plan = {}

    def put(step, b, *actions):
        plan.setdefault((step, b), []).extend(actions)

    def gate(step):
        pass_on(step).wait_recv()
        gate_block(sums, gate_own, gate_mate, step)

    def out(step):
        out_block(sums, out_own, out_mate, step)

    def rest(t):
        sums.ring_go(t, 0, "far_right", "far_left", "near_right", "near_left")

    put(0, 0, *[load.wait for load in loads[:4]])
    put(0, 2, *[load.wait for load in loads[4:]])
    for b, (action, step) in enumerate(((out, 2), (out, 1), (gate, 2), (out, 3), (gate, 1), (out, 0), (gate, 3), (gate, 0))):
        put(0, b, part(action, step))
    put(0, 5, part(rest, 3))
    put(0, 7, part(rest, 2))
    put(1, 1, part(sums.relay, 1, 0))
    put(1, 4, part(sums.relay, 0, 0))
    put(2, 1, part(sums.relay, 3, 0))
    put(2, 5, part(sums.relay, 2, 0))
    put(3, 3, part(sums.settle, 1, 0))
    put(3, 6, part(sums.settle, 0, 0))
    put(3, 7, part(sums.settle, 3, 0))
    put(4, 0, part(sums.settle, 2, 0), part(sums.relay, 1, 1))
    put(4, 4, part(sums.relay, 0, 1), part(sums.relay, 3, 1))
    put(4, 7, part(sums.settle, 1, 1), part(sums.relay, 2, 1))
    put(5, 2, part(sums.settle, 0, 1), part(sums.settle, 3, 1))
    put(5, 4, part(sums.relay, 1, 2), part(sums.settle, 2, 1))
    put(5, 7, part(sums.relay, 0, 2), part(sums.relay, 3, 2))
    put(6, 1, part(sums.share, 1))
    put(6, 2, part(sums.relay, 2, 2))
    put(6, 4, part(sums.share, 0), part(sums.share, 3))
    put(6, 7, part(sums.share, 2))
    for t, at in ((1, (7, 0)), (0, (7, 2)), (3, (7, 4)), (2, (7, 6))):
        put(*at, part(sums.paired, t), part(sums.spread_out, t, 0))
    for t, at in ((1, (7, 5)), (0, (7, 7)), (3, (8, 1)), (2, (8, 4))):
        put(*at, part(sums.spread_on, t, 0))
    return plan


def core_back(xc, xr, raw, dt, cs, state, total, y, dys, own, start, decay, heads, kernel, *factors):
    f = lambda *s: jax.ShapeDtypeStruct(s, F32)
    b = lambda *s: jax.ShapeDtypeStruct(s, BF16)
    both = lambda i: jnp.where(i < 2 * CHUNKS, lax.rem(i, CHUNKS), CHUNKS - 1)
    late = lambda i: jnp.clip(i - CHUNKS, 0, CHUNKS - 1)
    following = lambda i: jnp.clip(i - CHUNKS + 1, 1, CHUNKS - 1)
    lagging = lambda i: jnp.maximum(i - CHUNKS - 1, 0)
    return pl.pallas_call(
        core_back_body,
        grid=(2 * CHUNKS + 1,),
        in_specs=[
            chunked(CONV, both), once(TOK + HALO, CONV), chunked(128, late), chunked(128, both), chunked(128, both), once(TOK, 128),
            chunked(DI, both), chunked(DI, following), once(N, DI), chunked(DI, late), chunked(DI, both),
            pl.BlockSpec(memory_space=pl.ANY), once(N, DI), once(8, DI), once(8, 128), once(8, CONV),
            *[pl.BlockSpec(memory_space=pl.ANY)] * 7,
        ],
        out_specs=[
            chunked(CONV, lagging), chunked(128, late), whole(8, CONV), whole(8, 128),
            *[pl.BlockSpec(memory_space=pl.ANY)] * 6,
        ],
        out_shape=[
            b(TOK, CONV), b(TOK, 128), f(8, CONV), f(8, 128), *[f(*kept_shape(o, r)) for o, r in zip(*EARLY[:2])],
            b(TOK, CONV), b(TOK, 128),
        ],
        scratch_shapes=[
            pltpu.VMEM((D, TOK), BF16), pltpu.VMEM((DI, TOK), BF16), pltpu.VMEM((TOK, D), BF16), pltpu.VMEM((TOK, DI), BF16),
            pltpu.VMEM((D // 2, TOK), BF16), pltpu.VMEM((DI // 2, TOK), BF16), pltpu.VMEM((TOK, D), BF16),
            pltpu.SemaphoreType.DMA((7,)),
            pltpu.VMEM((TOK, DI), BF16), pltpu.VMEM((2, Q, CONV), BF16), pltpu.VMEM((TOK, 128), BF16),
            pltpu.SemaphoreType.DMA((9,)), pltpu.SemaphoreType.DMA((9,)), pltpu.SemaphoreType.DMA((CHUNKS - 1,)),
            pltpu.VMEM((128, DI), BF16), pltpu.VMEM((DI, 128), BF16), pltpu.VMEM((CHUNKS, N, DI), F32),
            pltpu.VMEM((CHUNKS, Q, DI), F32), pltpu.VMEM((CHUNKS, Q, 2 * N), F32), pltpu.VMEM((2, Q, CONV), F32),
            pltpu.VMEM((8, CONV), F32), pltpu.VMEM((8, CONV), F32), pltpu.VMEM((8, CONV), F32), pltpu.SemaphoreType.DMA, pltpu.SemaphoreType.DMA,
            *HAND_SCRATCH, *sums_scratch(*EARLY),
        ],
        compiler_params=pltpu.CompilerParams(collective_id=3, has_side_effects=True, vmem_limit_bytes=LIMIT),
        cost_estimate=pl.CostEstimate(flops=12 * 10**9, bytes_accessed=40 * 10**6, transcendentals=4 * 10**6),
        name="core_back",
    )(xc, xr, raw, dt, cs, cs, state, state, total, y, dys, own, start, decay, heads, kernel, *factors)


COLS = DI + CONV + H
PARTS = ((448, 448, 400), (64, 64, 0))
SMALL_ROWS = 48


def gather_body(in_ref, out_ref, small_ref, in_all, out_all, small_all, wide_in, wide_out, own_in, own_out,
                load_sem, x_send, x_recv, ring_send, ring_recv, mate_send, mate_recv, small_send, small_recv, keep_sem):
    here = my_place()
    core, x_lo = here["core"], lax.rem(here["x"], 2)
    mine = x_lo * 2 + core
    far = (1 - x_lo) * 2 + core
    sibling = device_at({**here, "core": 1 - core})
    right = {a: device_at(moved(here, a, 1)) for a in "xyz"}
    left = {a: device_at(moved(here, a, 3)) for a in "xyz"}
    loads = [
        pltpu.make_async_copy(in_ref, wide_in, load_sem.at[0]),
        pltpu.make_async_copy(out_ref, wide_out, load_sem.at[1]),
    ]
    for load in loads:
        load.start()
    barrier = pltpu.get_barrier_semaphore()
    partners = [sibling] + [right[a] for a in "xyz"] + [left[a] for a in "xyz"]
    for partner in partners:
        pl.semaphore_signal(barrier, inc=1, device_id=partner, device_id_type=MESH_ID)
    pl.semaphore_wait(barrier, len(partners))

    own, whole = (own_in, own_out), (in_all, out_all)
    started = []

    def remote(src, dst, send, recv, target):
        return pltpu.make_async_remote_copy(
            src_ref=src, dst_ref=dst, send_sem=send, recv_sem=recv,
            device_id=target, device_id_type=MESH_ID,
        )

    def go(copy):
        copy.start()
        started.append(copy)

    def rows(a, part, by, half):
        size = PARTS[a][part]
        base = (0, 4 * PARTS[a][0], 4 * PARTS[a][0] + 4 * PARTS[a][1])[part]
        if part < 2:
            base = base + lax.rem(here["yz"[part]] + by, 4) * size
            count = size if half is None else size // 2
            if half:
                base = base + size // 2
        else:
            count = 2 * size if half is None else size
            if half:
                base = base + size
        return pl.ds(pl.multiple_of(base, 16), count)

    def x_copy(a, part, side):
        at = rows(a, part, 0, side)
        target = left["x"] if side else right["x"]
        return remote(own[a].at[at], whole[a].at[mine, at], x_send.at[a, part, side], x_recv.at[a, part, side], target)

    def x_wait(a, part):
        for side in range(2):
            at = rows(a, part, 0, side)
            remote(own[a].at[at], whole[a].at[far, at], x_send.at[a, part, side], x_recv.at[a, part, side], sibling).wait_recv()

    def to_mate(a, at, k):
        piece = whole[a].at[far, at]
        go(remote(piece, piece, mate_send.at[a, k], mate_recv.at[a, k], sibling))

    def ring_copy(a, part, by, half, k, target):
        piece = whole[a].at[far, rows(a, part, by, half)]
        return remote(piece, piece, ring_send.at[a, part, k], ring_recv.at[a, part, k], target)

    small_copies = []
    for k, target in enumerate((sibling, right["x"], sibling)):
        source = small_ref if k < 2 else small_all.at[far]
        place = mine if k < 2 else far
        small_copies.append(remote(source, small_all.at[place], small_send.at[k], small_recv.at[k], target))
    go(small_copies[0])
    go(small_copies[1])

    keeps = [
        pltpu.make_async_copy(own_in, in_all.at[mine], keep_sem.at[0]),
        pltpu.make_async_copy(own_out, out_all.at[mine], keep_sem.at[1]),
        pltpu.make_async_copy(small_ref, small_all.at[mine], keep_sem.at[2]),
    ]
    loads[0].wait()

    def narrow_in(i, carry):
        at = pl.ds(pl.multiple_of(i * 32, 32), 32)
        own_in[at, :] = wide_in[at, :].astype(BF16)
        return carry

    lax.fori_loop(0, COLS // 32, narrow_in, 0)
    for part in (0, 1):
        for side in range(2):
            go(x_copy(0, part, side))
    loads[1].wait()

    def narrow_out(i, carry):
        at = pl.ds(pl.multiple_of(i * 16, 16), 16)
        own_out[at, :] = wide_out[at, :].astype(BF16)
        return carry

    lax.fori_loop(0, 512 // 16, narrow_out, 0)
    for part in (0, 1):
        for side in range(2):
            go(x_copy(1, part, side))
    for side in range(2):
        go(x_copy(0, 2, side))
    for a in range(2):
        go(remote(own[a], whole[a].at[mine], mate_send.at[a, 0], mate_recv.at[a, 0], sibling))
    for keep in keeps:
        keep.start()

    for a in range(2):
        for part in (0, 1):
            axis = "yz"[part]
            x_wait(a, part)
            go(ring_copy(a, part, 0, None, 0, right[axis]))
            go(ring_copy(a, part, 0, None, 1, left[axis]))
            to_mate(a, rows(a, part, 0, None), 1 + 4 * part)
    remote(small_ref, small_all.at[far], small_send.at[1], small_recv.at[1], sibling).wait_recv()
    go(small_copies[2])
    for a in range(2):
        for part in (0, 1):
            axis = "yz"[part]
            ring_copy(a, part, 3, None, 0, right[axis]).wait_recv()
            go(ring_copy(a, part, 3, 0, 2, right[axis]))
            to_mate(a, rows(a, part, 3, None), 2 + 4 * part)
            ring_copy(a, part, 1, None, 1, left[axis]).wait_recv()
            go(ring_copy(a, part, 1, 1, 3, left[axis]))
            to_mate(a, rows(a, part, 1, None), 3 + 4 * part)
    x_wait(0, 2)
    to_mate(0, rows(0, 2, 0, None), 9)
    for a in range(2):
        for part in (0, 1):
            axis = "yz"[part]
            ring_copy(a, part, 2, 0, 2, right[axis]).wait_recv()
            ring_copy(a, part, 2, 1, 3, left[axis]).wait_recv()
            to_mate(a, rows(a, part, 2, None), 4 + 4 * part)

    beside, beyond = x_lo * 2 + 1 - core, (1 - x_lo) * 2 + 1 - core
    for a in range(2):
        remote(own[a], whole[a].at[beside], mate_send.at[a, 0], mate_recv.at[a, 0], sibling).wait_recv()
        for part in (0, 1):
            for k, by in enumerate((0, 3, 1, 2)):
                piece = whole[a].at[beyond, rows(a, part, by, None)]
                remote(piece, piece, mate_send.at[a, 1 + 4 * part + k], mate_recv.at[a, 1 + 4 * part + k], sibling).wait_recv()
    piece = in_all.at[beyond, rows(0, 2, 0, None)]
    remote(piece, piece, mate_send.at[0, 9], mate_recv.at[0, 9], sibling).wait_recv()
    remote(small_ref, small_all.at[beside], small_send.at[0], small_recv.at[0], sibling).wait_recv()
    remote(small_ref, small_all.at[beyond], small_send.at[2], small_recv.at[2], sibling).wait_recv()
    for copy in started:
        copy.wait_send()
    for keep in keeps:
        keep.wait()


def gather_weights(in_turned, out_weight, small):
    hbm = pl.BlockSpec(memory_space=pl.ANY)
    dma = pltpu.SemaphoreType.DMA
    return pl.pallas_call(
        gather_body,
        out_shape=[
            jax.ShapeDtypeStruct((4, COLS, 256), BF16),
            jax.ShapeDtypeStruct((4, 512, D), BF16),
            jax.ShapeDtypeStruct((4, SMALL_ROWS, 128), BF16),
        ],
        in_specs=[hbm, hbm, pl.BlockSpec(memory_space=pltpu.VMEM)],
        out_specs=[hbm, hbm, hbm],
        scratch_shapes=[
            pltpu.VMEM((COLS, 256), F32), pltpu.VMEM((512, D), F32), pltpu.VMEM((COLS, 256), BF16), pltpu.VMEM((512, D), BF16),
            dma((2,)), dma((2, 3, 2)), dma((2, 3, 2)), dma((2, 2, 4)), dma((2, 2, 4)), dma((2, 10)), dma((2, 10)),
            dma((3,)), dma((3,)), dma((3,)),
        ],
        compiler_params=pltpu.CompilerParams(collective_id=4, has_side_effects=True, vmem_limit_bytes=LIMIT),
        name="gather_weights",
    )(in_turned, out_weight, small)


ROWS_IN = TOK + HALO
Z_BLOCKS = DI // WIDE
X_BLOCKS = CONV // WIDE


def project_body(rows_ref, gain_ref, weight_ref, tail_ref, z_ref, xr_ref, raw_ref, turned_ref, normed):
    step = pl.program_id(0)

    nt = ((1,), (1,))

    def times_weight(rows, weight):
        total = dot(rows[:, :256], weight[0], nt)
        for q in range(1, 4):
            total = total + dot(rows[:, q * 256 : (q + 1) * 256], weight[q], nt)
        return total

    @pl.when(step == 0)
    def _():
        for i in range(ROWS_IN // HALO):
            at = slice(i * HALO, (i + 1) * HALO)
            rows = rows_ref[at].astype(F32)
            square = jnp.sum(rows * rows, axis=1, keepdims=True) * (1.0 / D)
            normed[at] = (rows * lax.rsqrt(square + NORM_EPS) * gain_ref[0:1]).astype(BF16)
        raw_ref[...] = jnp.zeros_like(raw_ref)
        for c in range(CHUNKS):
            rows = normed[HALO + c * Q : HALO + (c + 1) * Q]
            raw_ref[c * Q : (c + 1) * Q, :H] = times_weight(rows, tail_ref)
            for i in range(D // Q):
                tile = rows[:, i * Q : (i + 1) * Q].astype(F32)
                turned_ref[i * Q : (i + 1) * Q, c * Q : (c + 1) * Q] = tile.T.astype(BF16)

    @pl.when(step < Z_BLOCKS)
    def _():
        z_ref[...] = times_weight(normed[HALO:], weight_ref)

    @pl.when(step >= Z_BLOCKS)
    def _():
        xr_ref[...] = times_weight(normed[...], weight_ref).astype(BF16)


def project(rows, gain, weight):
    return pl.pallas_call(
        project_body,
        grid=(Z_BLOCKS + X_BLOCKS,),
        in_specs=[
            pl.BlockSpec((ROWS_IN, D), lambda i: (0, 0)),
            pl.BlockSpec((1, D), lambda i: (0, 0)),
            pl.BlockSpec((4, WIDE, 256), lambda i: (0, i, 0)),
            pl.BlockSpec((4, H, 256), lambda i: (0, (DI + CONV) // H, 0)),
        ],
        out_specs=[
            pl.BlockSpec((TOK, WIDE), lambda i: (0, jnp.minimum(i, Z_BLOCKS - 1))),
            pl.BlockSpec((ROWS_IN, WIDE), lambda i: (0, jnp.maximum(i - Z_BLOCKS, 0))),
            pl.BlockSpec((TOK, 128), lambda i: (0, 0)),
            pl.BlockSpec((D, TOK), lambda i: (0, 0)),
        ],
        out_shape=[
            jax.ShapeDtypeStruct((TOK, DI), F32),
            jax.ShapeDtypeStruct((ROWS_IN, CONV), BF16),
            jax.ShapeDtypeStruct((TOK, 128), F32),
            jax.ShapeDtypeStruct((D, TOK), BF16),
        ],
        scratch_shapes=[pltpu.VMEM((ROWS_IN, D), BF16)],
        compiler_params=pltpu.CompilerParams(vmem_limit_bytes=LIMIT),
        cost_estimate=pl.CostEstimate(flops=5 * 10**9, bytes_accessed=20 * 10**6, transcendentals=0),
        name="project",
    )(rows, gain, weight, weight)


def finish_body(turned_far, mate_turned_far, rows_far, dz_far, dxr_far, mate_dxr_far, draw_ref, mate_draw, dkernel_ref, dgate_ref,
                dheads_ref, gain_ref, weight_ref, begun0, begun1, begun2, begun3, out0, out1, out2, grad_ref, small_ref,
                early0, early1, early2, early3,
                turned_ref, mate_turned, rows_ref, dz_ref, dxr_ref, mate_dxr, load_sem, steps, pack, near_pack, axis_pack, small_total, total, dgain, weights, tail, weight_sem, grad_sem,
                small_send, small_recv, near_send, near_recv, *scratch):
    sums = Sums(*LATE, (out0, out1, out2), scratch[:-2])
    early = Spread(*EARLY, (early0, early1, early2, early3), scratch[-2:])
    core, here = sums.core, sums.here
    own, mate = (turned_ref, dxr_ref), (mate_turned, mate_dxr)

    starts = [k * 512 for k in range(8)] + [8 * 512]
    counts = [512] * 8 + [WIDE]

    def fetch(k):
        return pltpu.make_async_copy(
            weight_ref.at[:, pl.ds(starts[k], counts[k])], weights.at[k % 2, :, pl.ds(0, counts[k])], weight_sem.at[k % 2]
        )

    tail_copy = pltpu.make_async_copy(weight_ref.at[:, pl.ds(DI + CONV, H)], tail, weight_sem.at[2])
    loads = {
        name: pltpu.make_async_copy(far, near, load_sem.at[k])
        for k, (name, far, near) in enumerate((
            ("turned", turned_far, turned_ref), ("mate_turned", mate_turned_far, mate_turned), ("dxr", dxr_far, dxr_ref),
            ("mate_dxr", mate_dxr_far, mate_dxr), ("dz", dz_far, dz_ref), ("rows", rows_far, rows_ref),
        ))
    }
    for load in loads.values():
        load.start()
    tail_copy.start()
    fetch(0).start()
    fetch(1).start()
    greet_all(sums.greet() + [device_at(moved(here, a, 2)) for a in "yz"])

    def input_step(k):
        fetch(k).wait()
        source = dz_ref if k < 4 else dxr_ref
        first = starts[k] if k < 4 else starts[k] - DI
        columns = source[:, first : first + counts[k]]
        for q in range(4):
            lanes = slice(q * 256, (q + 1) * 256)
            total[:, lanes] += dot(columns, weights[k % 2, q, : counts[k]])
        if k + 2 < len(starts):
            fetch(k + 2).start()

    def input_end():
        def some(i, carry):
            at = pl.ds(pl.multiple_of(i * 32, 32), 32)
            rows = rows_ref[at, :].astype(F32)
            dn = total[at, :]
            scale = lax.rsqrt(jnp.sum(rows * rows, axis=1, keepdims=True) * (1.0 / D) + NORM_EPS)
            dgain[0:1] += jnp.sum(dn * rows * scale, axis=0, keepdims=True)
            dn = dn * gain_ref[0:1]
            pull = jnp.sum(dn * rows, axis=1, keepdims=True) * (1.0 / D) * scale * scale * scale
            total[at, :] = scale * dn - rows * pull
            return carry

        dgain[...] = jnp.zeros_like(dgain)
        lax.fori_loop(0, TOK // 32, some, 0)


    def small_begin():
        pack[...] = jnp.zeros_like(pack)
        pack[0:5] = dkernel_ref[0:5]
        pack[5:6, :DI] = dgate_ref[0:1]
        pack[6:7, :D] = dgain[0:1]
        for k in range(3):
            pack[6:7, D + k * 128 : D + (k + 1) * 128] = dheads_ref[k : k + 1]
        near_pack[core] = pack[...]
        near_copy().start()

    def near_copy():
        return remote(pack, near_pack.at[core], near_send, near_recv, sums.sibling)

    def axis_copy(k, by):
        a = "xyz"[k]
        source = small_total.at[k]
        target = device_at(moved(here, a, by))
        return remote(source, axis_pack.at[k, here[a]], small_send.at[k, by - 1], small_recv.at[k, by - 1], target)

    def small_axis(k):
        if k == 0:
            near_copy().wait_recv()
            value = near_pack[0] + near_pack[1]
        else:
            for by in range(1, 4):
                axis_copy(k - 1, by).wait_recv()
            value = (axis_pack[k - 1, 0] + axis_pack[k - 1, 1]) + (axis_pack[k - 1, 2] + axis_pack[k - 1, 3])
        small_total[k] = value
        if k < 3:
            axis_pack[k, here["xyz"[k]]] = value
            for by in range(1, 4):
                axis_copy(k, by).start()

    inner = (0, 1, 2)

    def each(method, *arguments):
        for t in inner:
            method(t, *arguments)

    def blocks(step):
        for t in inner:
            make_block(sums, t, functools.partial(inner_block, t, steps), own, mate, step)

    for t in (1, 0, 3, 2):
        early.spread_out(t, 1)
    loads["turned"].wait()
    loads["mate_turned"].wait()
    for x_lo in range(2):
        rows = pl.ds(pl.multiple_of((x_lo * 2 + core) * 256, 256), 256)
        steps[x_lo * 256 : (x_lo + 1) * 256] = dot(turned_ref[rows, :], draw_ref[...]) + dot(
            mate_turned[x_lo * 256 : (x_lo + 1) * 256], mate_draw[...]
        )
    loads["dxr"].wait()
    loads["mate_dxr"].wait()
    blocks(2)
    blocks(1)
    blocks(3)
    each(sums.relay, 0)
    for t in (1, 0, 3, 2):
        early.spread_on(t, 1)
    blocks(0)
    loads["dz"].wait()
    tail_copy.wait()
    for q in range(4):
        total[:, q * 256 : (q + 1) * 256] = dot(draw_ref[:, :H], tail[q])
    input_step(0)
    each(sums.settle, 0)
    input_step(1)
    input_step(2)
    each(sums.relay, 1)
    input_step(3)
    input_step(4)
    each(sums.settle, 1)
    input_step(5)
    each(sums.relay, 2)
    input_step(6)
    input_step(7)
    each(sums.share)
    input_step(8)
    loads["rows"].wait()
    input_end()
    small_begin()
    grad_copy = pltpu.make_async_copy(total, grad_ref, grad_sem)
    grad_copy.start()
    each(sums.paired)
    each(sums.spread_out, 0)
    small_axis(0)
    each(sums.spread_on, 0)
    small_axis(1)
    each(sums.arrive)
    each(sums.spread_out, 1)
    small_axis(2)
    for t in (1, 0, 3, 2):
        early.spread_end(t)
    small_axis(3)
    small_copy = pltpu.make_async_copy(small_total.at[3], small_ref, weight_sem.at[0])
    small_copy.start()
    each(sums.spread_on, 1)
    each(sums.spread_end)
    sums.close()
    early.close()
    near_copy().wait_send()
    for k in range(3):
        for by in range(1, 4):
            axis_copy(k, by).wait_send()
    small_copy.wait()
    grad_copy.wait()


def finish(turned, mate_turned, rows, dz, dxr, mate_dxr, draw, mate_draw, dkernel, dgate, dheads, gain, weight, *begun):
    f = lambda *s: pltpu.VMEM(s, F32)
    dma = pltpu.SemaphoreType.DMA
    scratch = [
        *[pltpu.VMEM(s, BF16) for s in ((D, TOK), (D // 2, TOK), (TOK, D), (TOK, DI), (TOK, CONV), (TOK, CONV))], dma((6,)),
        f(512, 128), f(8, CONV), f(2, 8, CONV), f(3, 4, 8, CONV), f(4, 8, CONV), f(TOK, D), f(8, D),
        pltpu.VMEM((2, 4, 512, 256), BF16), pltpu.VMEM((4, H, 256), BF16),
        dma((3,)), dma, dma((3, 3)), dma((3, 3)), dma, dma, *sums_scratch(*LATE), *spread_scratch(EARLY[2]),
    ]
    hbm = pl.BlockSpec(memory_space=pl.ANY)
    vmem = pl.BlockSpec(memory_space=pltpu.VMEM)
    kept = [jax.ShapeDtypeStruct(kept_shape(order, r), F32) for order, r in zip(*LATE[:2])]
    return pl.pallas_call(
        finish_body,
        out_shape=kept + [jax.ShapeDtypeStruct(shape, F32) for shape in ((TOK, D), (8, CONV), *[part.shape for part in begun])],
        in_specs=[hbm] * 6 + [vmem] * 6 + [hbm] * 5,
        out_specs=[hbm] * 9,
        input_output_aliases={13 + t: 5 + t for t in range(4)},
        scratch_shapes=scratch,
        compiler_params=pltpu.CompilerParams(collective_id=1, has_side_effects=True, vmem_limit_bytes=LIMIT),
        cost_estimate=pl.CostEstimate(flops=8 * 10**9, bytes_accessed=30 * 10**6, transcendentals=0),
        name="finish",
    )(turned, mate_turned, rows, dz, dxr, mate_dxr, draw, mate_draw, dkernel, dgate, dheads, gain, weight, *begun)


def adamw(weight, first_moment, second, gradient, step_rate, weight_decay):
    first_new = BETA_ONE * first_moment + (1.0 - BETA_ONE) * gradient
    second_new = BETA_TWO * second + (1.0 - BETA_TWO) * gradient * gradient
    first_hat = first_new * (step_rate / (1.0 - BETA_ONE**STEP))
    second_hat = second_new * (1.0 / (1.0 - BETA_TWO**STEP))
    weight_new = weight * (1.0 - step_rate * weight_decay) - first_hat / (jnp.sqrt(second_hat) + ADAM_EPS)
    return (weight_new, first_new, second_new)


IN_ROWS = 512


def in_update_body(tall_ref, short_ref, low_ref, middle_ref, high_ref, w_ref, m_ref, v_ref, w_out, m_out, v_out):
    step = pl.program_id(0)

    def update(rows, gradient):
        w, m, v = adamw(w_ref[rows], m_ref[rows], v_ref[rows], gradient, 0.05, 0.1)
        w_out[rows], m_out[rows], v_out[rows] = w, m, v

    def inner_tile(tile):
        which, k = tile // 6, tile % 6
        ref = (low_ref, middle_ref, high_ref)[which]
        height = 128 if which == 0 else 64
        parts = []
        for band in range(256 // height):
            at = k * height
            while at < (k + 1) * height:
                piece, row = at // 48, at % 48
                count = min(48 - row, (k + 1) * height - at)
                parts.append(ref[band, piece, row : row + count])
                at += count
        return jnp.concatenate(parts, axis=0)

    @pl.when(step < 4)
    def _():
        for tile in range(4):
            halves_ = [jnp.concatenate([tall_ref[0, hi, tile], short_ref[tile, 0, hi]], axis=0).T for hi in range(2)]
            update(slice(tile * 128, tile * 128 + 128), jnp.concatenate(halves_, axis=1))

    for s in range(4, 9):
        @pl.when(step == s)
        def _():
            for tile in range(4 if s < 8 else 2):
                update(slice(tile * 128, tile * 128 + 128), inner_tile(4 * (s - 4) + tile).T)
            if s == 8:
                pieces = jnp.concatenate([low_ref[band, i, 48:56] for band in range(2) for i in range(16)], axis=0)
                update(slice(256, 256 + H), pieces.T[:H])


def in_update(tall, short, low, middle, high, w, m, v):
    rows = pl.BlockSpec((IN_ROWS, 256), lambda i: (i, 0))
    shape = jax.ShapeDtypeStruct(w.shape, F32)
    return pl.pallas_call(
        in_update_body,
        grid=(9,),
        in_specs=[
            pl.BlockSpec((1, 2, 4, TALL, 128), lambda i: (jnp.minimum(i, 3), 0, 0, 0, 0)),
            pl.BlockSpec((4, 1, 2, SHORT, 128), lambda i: (0, jnp.minimum(i, 3), 0, 0, 0)),
            whole(2, 16, 64, 128), whole(4, 8, 48, 128), whole(4, 8, 48, 128),
            rows, rows, rows,
        ],
        out_specs=[rows, rows, rows],
        out_shape=[shape, shape, shape],
        compiler_params=pltpu.CompilerParams(vmem_limit_bytes=LIMIT),
        cost_estimate=pl.CostEstimate(flops=2 * 10**7, bytes_accessed=32 * 10**6, transcendentals=0),
        name="in_update",
    )(
        tall, short, low.reshape(2, 16, 64, 128), middle.reshape(4, 8, 48, 128), high.reshape(4, 8, 48, 128), w, m, v
    )


def out_update_body(tall_ref, short_ref, cot_ref, norm_ref, w_ref, m_ref, v_ref, w_out, m_out, v_out, grad_ref):
    grad_ref[...] = cot_ref[...].astype(F32) + norm_ref[...]
    for tile in range(8):
        lanes = slice(tile * 128, tile * 128 + 128)
        hi, y = tile // 4, tile % 4
        gradient = jnp.concatenate([tall_ref[hi, y, 0], short_ref[y, 0, hi]], axis=0)
        w, m, v = adamw(w_ref[:, lanes], m_ref[:, lanes], v_ref[:, lanes], gradient, 0.05, 0.1)
        w_out[:, lanes], m_out[:, lanes], v_out[:, lanes] = w, m, v


def out_update(tall, short, cot, norm, w, m, v):
    rows = pl.BlockSpec((128, D), lambda i: (i, 0))
    shape = jax.ShapeDtypeStruct(w.shape, F32)
    return pl.pallas_call(
        out_update_body,
        grid=(4,),
        in_specs=[
            pl.BlockSpec((2, 4, 1, TALL, 128), lambda i: (0, 0, i, 0, 0)),
            pl.BlockSpec((4, 1, 2, SHORT, 128), lambda i: (0, i, 0, 0, 0)),
            rows, rows, rows, rows, rows,
        ],
        out_specs=[rows, rows, rows, rows],
        out_shape=[shape, shape, shape, jax.ShapeDtypeStruct((TOK, D), F32)],
        compiler_params=pltpu.CompilerParams(vmem_limit_bytes=LIMIT),
        cost_estimate=pl.CostEstimate(flops=2 * 10**7, bytes_accessed=16 * 10**6, transcendentals=0),
        name="out_update",
    )(tall, short, cot, norm, w, m, v)


def shifted(block, axis, distance):
    devices = range(lax.axis_size(axis))
    route = [(i - distance, i) for i in devices if i - distance in devices]
    return lax.ppermute(block, axis, route)


def small_rows(conv, gains, heads):
    conv = jnp.pad(conv, ((0, 0), (0, 64))).reshape(25, 128)
    heads = jnp.pad(heads, ((0, 0), (0, 120)))
    joined = jnp.concatenate([conv, gains.reshape(6, 128), heads], axis=0)
    return jnp.pad(joined, ((0, SMALL_ROWS - 34), (0, 0)))


def small_wholes(rows):
    conv = rows[:, :25].reshape(4, 5, 640)[:, :, :576]
    conv = jnp.transpose(conv, (1, 0, 2)).reshape(5, CONV)
    heads = jnp.transpose(rows[:, 31:34, :8], (1, 0, 2)).reshape(3, H)
    return conv, rows[:, 25:31].reshape(1, D + DI), heads


def small_totals(small):
    shard = lax.axis_index("shard")
    conv = lax.dynamic_slice(small, (0, shard * 576), (5, 576))
    gains = jnp.concatenate([small[6, :D], small[5, :DI]], axis=0)
    heads = small[6, D : D + 384].reshape(3, 128)
    return conv, lax.dynamic_slice(gains, (shard * 768,), (768,)), lax.dynamic_slice(heads, (0, shard * 8), (3, 8))


def on_device(
    hidden_in, cotangent, in_weight, in_first, in_second, out_weight, out_first, out_second, conv_weight, conv_first,
    conv_second, norm_gains, gains_first, gains_second, head_params, head_first, head_second,
):
    rows_in = hidden_in.reshape(TOK, D)
    cot_rows = cotangent.reshape(TOK, D)
    in_full, out_full, small = gather_weights(
        in_weight.T, out_weight, small_rows(conv_weight, norm_gains, head_params).astype(BF16)
    )
    out_full = out_full.reshape(DI, D)
    conv_full, gain_full, head_full = small_wholes(small.astype(F32))
    kernel = jnp.pad(conv_full, ((0, 3), (0, 0)))
    heads = jnp.pad(head_full, ((0, 5), (0, 96)))
    gain_in, gain_gate = gain_full[:, :D], gain_full[:, D:]
    halo = shifted(rows_in[TOK - HALO :], "shard", 1)

    z, xr, raw, normed_turned = project(jnp.concatenate([halo, rows_in], axis=0), gain_in, in_full)
    xc, dt, cs, local, end, decay = chunk_states(xr, raw, kernel, heads)
    y, state, gated, gated_turned, total = outputs(xc, dt, cs, local, end, decay, z, heads, gain_gate)
    branch_out = jnp.dot(gated, out_full, preferred_element_type=F32)
    block_out = (rows_in.astype(F32) + branch_out).astype(BF16)

    nt = (((1,), (1,)), ((), ()))
    grad_gated = lax.dot_general(cot_rows, out_full, nt, preferred_element_type=F32)
    dys, dz, own, start, dgain_gate, mate_gated, mate_turned, mate_cot = gate_back(
        grad_gated, y, z, xc, cs, gain_gate, gated_turned, normed_turned, cot_rows
    )
    dxr, draw, dkernel, dheads, *begun, mate_dxr, mate_draw = core_back(
        xc, xr, raw, dt, cs, state, total, y, dys, own, start, decay, heads, kernel,
        normed_turned, gated_turned, cot_rows, dz, mate_turned, mate_gated, mate_cot,
    )
    *inner_totals, grad_norm, small, gate_tall, out_tall, gate_short, out_short = finish(
        normed_turned, mate_turned, rows_in, dz, dxr, mate_dxr, draw, mate_draw, dkernel, dgain_gate, dheads, gain_in,
        in_full, *begun,
    )
    in_new = in_update(gate_tall, gate_short, *inner_totals, in_weight.T, in_first.T, in_second.T)
    in_new = [part.T for part in in_new]
    *out_new, grad_input = out_update(out_tall, out_short, cot_rows, grad_norm, out_weight, out_first, out_second)
    conv_total, gains_total, heads_total = small_totals(small)
    conv_new = adamw(conv_weight, conv_first, conv_second, conv_total, 0.3, 0.1)
    gains_new = adamw(norm_gains, gains_first, gains_second, gains_total, 0.5, 0.0)
    head_new = adamw(head_params, head_first, head_second, heads_total, 1.0, 0.0)
    return (block_out.reshape(1, TOK, D), grad_input.reshape(1, TOK, D), *in_new, *out_new, *conv_new, *gains_new, *head_new)


def solution(mesh):
    in_specs = (
        P("rep", "shard", None),
        P("rep", "shard", None),
        P("shard", None),
        P("shard", None),
        P("shard", None),
        P("shard", None),
        P("shard", None),
        P("shard", None),
        P(None, "shard"),
        P(None, "shard"),
        P(None, "shard"),
        P("shard"),
        P("shard"),
        P("shard"),
        P(None, "shard"),
        P(None, "shard"),
        P(None, "shard"),
    )
    out_specs = (
        P("rep", "shard", None),
        P("rep", "shard", None),
        P("shard", None),
        P("shard", None),
        P("shard", None),
        P("shard", None),
        P("shard", None),
        P("shard", None),
        P(None, "shard"),
        P(None, "shard"),
        P(None, "shard"),
        P("shard"),
        P("shard"),
        P("shard"),
        P(None, "shard"),
        P(None, "shard"),
        P(None, "shard"),
    )
    return jax.shard_map(
        on_device, mesh=mesh, in_specs=in_specs, out_specs=out_specs, check_vma=False
    )
```
